32 devices in a mesh: ctx: 16 (over z, y, core), head: 2 (over x).
Axes of the slice: x: 2, y: 2, z: 4, core: 2. Of those that a mesh axis runs over, the one named last changes fastest.
Arguments:
- query1: bfloat16 [8192, 6144], P('ctx', 'head'), may hold values from -6 to 6
- key1: bfloat16 [8192, 6144], P('ctx', 'head'), may hold values from -6 to 6
- value1: bfloat16 [8192, 6144], P('ctx', 'head'), may hold values from -50 to 50
- log_decay: float32 [8192, 64], P('ctx', 'head'), may hold values from -1 to 0
- out_weight: bfloat16 [6144, 3072], P('head'), may hold values from -0.078125 to 0.078125
- query2: bfloat16 [8192, 6144], P('ctx', 'head'), may hold values from -12 to 12
- key2: bfloat16 [8192, 6144], P('ctx', 'head'), may hold values from -6 to 6
- value2: bfloat16 [8192, 6144], P('ctx', 'head'), may hold values from -6 to 6
Outputs:
- linear_mixed: bfloat16 [8192, 3072], P(('ctx', 'head'))
- attended: bfloat16 [8192, 6144], P('ctx', 'head')
The draws below stay inside these ranges and needn't reach their ends.
All inputs are finite; a program needn't handle non-finite values.
Results may differ from the reference program's by a relative error of at most 0.017.
Values may be sent and summed in bfloat16 or wider, within the bound.
No kernel may reach another device: no remote copies, remote signals or barrier semaphores. Data moves between devices by JAX's collectives and lax.ppermute only.
A program may use at most 320 MiB of HBM per device.

```python
import math
import jax
import jax.numpy as jnp
from jax import lax

HEAD_TOTAL = 64
DH = 96
LBLOCK = 256
PROJ = 3072
TOK_DEV = 512
TOKEN_TOTAL = 8192
WINDOW = 1536


def clipped_normal(key, shape, bound):
    return jnp.clip(jax.random.normal(key, shape, jnp.float32), -bound, bound)


def draw_query2(key, part):
    values = clipped_normal(jax.random.fold_in(key, 1), (TOKEN_TOTAL, HEAD_TOTAL * DH), 6.0)
    return values.astype(jnp.bfloat16)


def draw_key2(key, part):
    values = clipped_normal(jax.random.fold_in(key, 3), (TOKEN_TOTAL, HEAD_TOTAL * DH), 6.0)
    return values.astype(jnp.bfloat16)


def draw_value1(key, part):
    column_scale = jnp.exp(jax.random.uniform(jax.random.fold_in(key, 21), (1, HEAD_TOTAL * DH), jnp.float32, -1.15, 1.15))
    row_scale = jnp.exp(jax.random.uniform(jax.random.fold_in(key, 22), (TOKEN_TOTAL, 1), jnp.float32, -1.15, 1.15))
    values = clipped_normal(jax.random.fold_in(key, 25), (TOKEN_TOTAL, HEAD_TOTAL * DH), 5.0)
    return (values * column_scale * row_scale).astype(jnp.bfloat16)


def draw_log_decay(key, part):
    fast_share = 0.35
    fast = jax.random.uniform(jax.random.fold_in(key, 31), (HEAD_TOTAL,), jnp.float32) < fast_share
    fast_rate = math.log(10.0) * jax.random.uniform(jax.random.fold_in(key, 32), (HEAD_TOTAL,), jnp.float32, 1.0 / 50.0, 1.0 / 30.0)
    slow_log = jax.random.uniform(jax.random.fold_in(key, 33), (HEAD_TOTAL,), jnp.float32, math.log(1.0 / 32.0), math.log(1.0 / 8.0))
    slow_rate = math.log(10.0) / TOKEN_TOTAL * jnp.exp(slow_log)
    baseline_speed = jnp.where(fast, fast_rate, slow_rate)
    processor_multiplier = jnp.exp(jax.random.uniform(jax.random.fold_in(key, 34), (TOKEN_TOTAL // TOK_DEV, HEAD_TOTAL), jnp.float32, -0.7, 0.7))
    processor_multiplier = jnp.repeat(processor_multiplier, TOK_DEV, axis=0)
    token_multiplier = jax.random.uniform(jax.random.fold_in(key, 35), (TOKEN_TOTAL, HEAD_TOTAL), jnp.float32, 0.5, 1.5)
    spike_amount = jax.random.uniform(jax.random.fold_in(key, 36), (TOKEN_TOTAL, HEAD_TOTAL), jnp.float32) < 4.0 / TOKEN_TOTAL
    spike_penalty = jnp.log(jax.random.uniform(jax.random.fold_in(key, 37), (TOKEN_TOTAL, HEAD_TOTAL), jnp.float32, 0.5, 0.8))
    return -(baseline_speed[None, :] * processor_multiplier * token_multiplier) + jnp.where(spike_amount, spike_penalty, 0.0)


def block_levels(key, shape, cuts, smallest, top_value):
    factor_of = 1.0
    for dim, blocks in cuts:
        steps = jax.random.uniform(jax.random.fold_in(jax.random.fold_in(key, 6), dim), (blocks,), jnp.float32, smallest / len(cuts), top_value / len(cuts))
        factor_of = factor_of * jnp.repeat(jnp.exp(steps), shape[dim] // blocks).reshape((-1,) + (1,) * (len(shape) - 1 - dim))
    return factor_of


def normal_values(own_key, shape, spread, limit, split=(), held_as=jnp.bfloat16):
    array = jax.random.normal(own_key, shape, jnp.float32) * spread
    if len(split) > 0:
        array = block_levels(own_key, shape, split, -0.22, 0.18) * array
    return jnp.clip(array, min=-limit, max=limit).astype(held_as)


def setup_inputs(seed: int = 0) -> dict:
    keys = jax.random.split(jax.random.key(seed), 9)
    return {
        "query1": normal_values(keys[0], (TOKEN_TOTAL, HEAD_TOTAL * DH), 1.0, 6.0, ((0, 16), (1, 2))),
        "key1": normal_values(keys[1], (TOKEN_TOTAL, HEAD_TOTAL * DH), 1.0, 6.0, ((0, 16), (1, 2))),
        "value1": draw_value1(jax.random.fold_in(keys[8], 71), 0),
        "log_decay": draw_log_decay(jax.random.fold_in(keys[8], 71), 0),
        "out_weight": normal_values(keys[4], (HEAD_TOTAL * DH, PROJ), (HEAD_TOTAL * DH) ** -0.5, 0.078125, ((0, 2),)),
        "query2": draw_query2(jax.random.fold_in(keys[8], 71), 0),
        "key2": draw_key2(jax.random.fold_in(keys[8], 71), 0),
        "value2": normal_values(keys[7], (TOKEN_TOTAL, HEAD_TOTAL * DH), 1.0, 6.0, ((0, 16), (1, 2))),
    }


eps_norm = 1e-06

def block_scan(carry_state, pieces):
    query_part = pieces[0].astype(jnp.float32)
    key_part = pieces[1].astype(jnp.float32)
    value_part = pieces[2].astype(jnp.float32)
    decay_part = pieces[3]
    block_len = decay_part.shape[0]
    running = jnp.cumsum(decay_part, axis=0)
    by_head = running.T
    gaps_log = by_head[:, :, None] - by_head[:, None, :]
    causal = jnp.arange(block_len)[:, None] >= jnp.arange(block_len)[None, :]
    weight = jnp.exp(jnp.where(causal[None], gaps_log, -jnp.inf))
    scores = jnp.einsum('ihd,jhd->hij', query_part, key_part)
    mixing = (scores * weight).astype(jnp.bfloat16)
    mixing = lax.optimization_barrier(mixing).astype(jnp.float32)
    inside = jnp.einsum('hij,jhd->ihd', mixing, value_part)
    outside = jnp.einsum('ihd,hde->ihe', query_part * jnp.exp(running)[:, :, None], carry_state, precision=lax.Precision.HIGHEST)
    block_total = running[-1]
    update = jnp.einsum('jhd,jhe->hde', key_part * jnp.exp(block_total[None, :] - running)[:, :, None], value_part, precision=lax.Precision.HIGHEST)
    new_state = jnp.exp(block_total)[:, None, None] * carry_state + update
    return (new_state, inside + outside)

def reference(query1, key1, value1, log_decay, out_weight, query2, key2, value2):
    block_count = TOKEN_TOTAL // LBLOCK
    inputs = (query1.reshape(block_count, LBLOCK, HEAD_TOTAL, DH), key1.reshape(block_count, LBLOCK, HEAD_TOTAL, DH), value1.reshape(block_count, LBLOCK, HEAD_TOTAL, DH), log_decay.reshape(block_count, LBLOCK, HEAD_TOTAL))
    final_state, outputs = lax.scan(block_scan, jnp.zeros((HEAD_TOTAL, DH, DH), jnp.float32), inputs)
    combined = outputs.reshape(TOKEN_TOTAL, HEAD_TOTAL, DH)
    mean_square = lax.optimization_barrier(jnp.mean(combined * combined, axis=-1, keepdims=True))
    normed = (combined / jnp.sqrt(mean_square + eps_norm)).astype(jnp.bfloat16).reshape(TOKEN_TOTAL, HEAD_TOTAL * DH)
    linear_mixed = jnp.dot(normed, out_weight, preferred_element_type=jnp.float32).astype(jnp.bfloat16)
    query_rows = min(512, TOK_DEV)
    key_span = WINDOW + query_rows
    padded_keys = jnp.pad(key2, ((WINDOW, 0), (0, 0)))
    padded_values = jnp.pad(value2, ((WINDOW, 0), (0, 0)))
    score_scale = 1.0 / math.sqrt(DH)

    def attend_block(block_index):
        first_row = (block_index * query_rows).astype(jnp.int32)
        query_part = lax.dynamic_slice_in_dim(query2, first_row, query_rows, 0).reshape(query_rows, HEAD_TOTAL, DH)
        key_part = lax.dynamic_slice_in_dim(padded_keys, first_row, key_span, 0).reshape(key_span, HEAD_TOTAL, DH)
        value_part = lax.dynamic_slice_in_dim(padded_values, first_row, key_span, 0).reshape(key_span, HEAD_TOTAL, DH)
        scores = jnp.einsum('ihd,jhd->hij', query_part.astype(jnp.float32), key_part.astype(jnp.float32)) * score_scale
        query_pos = first_row + jnp.arange(query_rows, dtype=jnp.int32)[:, None]
        key_pos = first_row - WINDOW + jnp.arange(key_span, dtype=jnp.int32)[None, :]
        allowed = (key_pos <= query_pos) & (query_pos - key_pos < WINDOW) & (key_pos >= 0)
        scores = jnp.where(allowed[None], scores, -jnp.inf)
        row_peak = lax.optimization_barrier(jnp.max(scores, axis=-1, keepdims=True))
        exponent = jnp.exp(scores - row_peak)
        probability = (exponent / lax.optimization_barrier(jnp.sum(exponent, axis=-1, keepdims=True))).astype(jnp.bfloat16)
        result = jnp.einsum('hij,jhd->ihd', probability.astype(jnp.float32), value_part.astype(jnp.float32))
        return result.astype(jnp.bfloat16).reshape(query_rows, HEAD_TOTAL * DH)
    attended = lax.map(attend_block, jnp.arange(TOKEN_TOTAL // query_rows, dtype=jnp.int32)).reshape(TOKEN_TOTAL, HEAD_TOTAL * DH)
    return (linear_mixed, attended)
```

```python
import functools
import math

import jax
import jax.numpy as jnp
from jax import lax
from jax.experimental import pallas as pl
from jax.experimental.pallas import tpu as pltpu
from jax.sharding import PartitionSpec as P

DH = 96
SUB = 256
BUNDLE = 4
WIDE = BUNDLE * DH
LANES = 128
EPS_NORM = 1e-06
VMEM_BYTES = 44 * 1024 * 1024
WINDOWS = ((0, 128, 0), (0, 256, 96), (128, 256, 64), (256, 128, 32))


def head_lanes(shape, start):
    lane = lax.broadcasted_iota(jnp.int32, shape, len(shape) - 1)
    return (lane >= start) & (lane < start + DH)


def pack_kernel(key_ref, value_ref, *rest):
    out_ref = rest[-1]
    out_ref[0] = key_ref[...]
    out_ref[1] = value_ref[...]


def pack(key, value, base, bundles, deps):
    rows = key.shape[0]
    block = pl.BlockSpec((rows, WIDE), lambda b: (0, base + b))
    return pl.pallas_call(
        pack_kernel,
        grid=(bundles,),
        in_specs=[block, block] + [pl.BlockSpec(memory_space=pl.ANY)] * len(deps),
        out_specs=pl.BlockSpec((2, rows, WIDE), lambda b: (0, 0, b)),
        out_shape=jax.ShapeDtypeStruct((2, rows, bundles * WIDE), key.dtype),
        compiler_params=pltpu.CompilerParams(vmem_limit_bytes=VMEM_BYTES),
        cost_estimate=pl.CostEstimate(
            flops=0, bytes_accessed=8 * rows * bundles * WIDE, transcendentals=0
        ),
        name="pack",
    )(key, value, *deps)


def attend_body(exists, query_ref, slots, out_ref):
    rows = query_ref.shape[0]
    scale = math.log2(math.e) / math.sqrt(DH)
    row = lax.broadcasted_iota(jnp.int32, (SUB, SUB), 0)
    col = lax.broadcasted_iota(jnp.int32, (SUB, SUB), 1)
    newer, older = col > row, col <= row
    low = jnp.float32(-1e30)
    parts = rows // SUB
    for part in range(parts):
        first = part * SUB
        spans = [(first, rows), (0, rows), (0, rows), (0, first + SUB)]
        total = None
        for start, width, place in WINDOWS:
            lanes = slice(start, start + width)
            query = query_ref[first : first + SUB, lanes]
            query = jnp.where(head_lanes(query.shape, place), query, jnp.zeros_like(query))
            scores, peak = [], None
            for slot in range(4):
                key_ref = slots[slot][0]
                span = spans[slot]
                score = lax.dot_general(
                    query,
                    key_ref[span[0] : span[1], lanes],
                    (((1,), (1,)), ((), ())),
                    preferred_element_type=jnp.float32,
                )
                if slot == 0:
                    edge = jnp.where(newer, score[:, :SUB], low)
                    score = (
                        jnp.concatenate([edge, score[:, SUB:]], axis=1)
                        if score.shape[1] > SUB
                        else edge
                    )
                if slot == 3:
                    cut = score.shape[1] - SUB
                    edge = jnp.where(older, score[:, cut:], low)
                    score = jnp.concatenate([score[:, :cut], edge], axis=1) if cut else edge
                scores.append(score)
                top = jnp.max(score, axis=1, keepdims=True)
                if slot < 3:
                    top = jnp.where(exists[slot], top, low)
                peak = top if peak is None else jnp.maximum(peak, top)
            result = None
            for slot in range(4):
                span = spans[slot]
                shift = peak * scale
                if slot < 3:
                    shift = jnp.where(exists[slot], shift, jnp.float32(1e30))
                weight = jnp.exp2(scores[slot] * scale - shift).astype(jnp.bfloat16)
                value = slots[slot][1][span[0] : span[1], lanes]
                value = jnp.where(head_lanes(value.shape, place), value, jnp.ones_like(value))
                term = jnp.dot(weight, value, preferred_element_type=jnp.float32)
                result = term if result is None else result + term
            spare = 96 if place == 0 else 0
            result = result * (1.0 / result[:, spare : spare + 1])
            result = jnp.where(head_lanes(result.shape, place), result, 0.0)
            pads = []
            if start:
                pads.append(jnp.zeros((SUB, start), jnp.float32))
            pads.append(result)
            if start + width < WIDE:
                pads.append(jnp.zeros((SUB, WIDE - start - width), jnp.float32))
            result = jnp.concatenate(pads, axis=1) if len(pads) > 1 else result
            total = result if total is None else total + result
        out_ref[first : first + SUB, :] = total.astype(out_ref.dtype)


def attend_kernel(info, query_ref, key_ref, value_ref, near_ref, mid_ref, swap_ref, *rest):
    out_ref = rest[-1]
    position = info[0]
    exists = [position >= 3, position >= 2, position >= 1]
    own = (key_ref, value_ref)
    near, mid, swap = [(r.at[0], r.at[1]) for r in (near_ref, mid_ref, swap_ref)]
    core = lax.rem(position, 2)

    @pl.when(core == 0)
    def _():
        attend_body(exists, query_ref, [near, mid, swap, own], out_ref)

    @pl.when(core == 1)
    def _():
        attend_body(exists, query_ref, [swap, mid, near, own], out_ref)


def attend(info, query, key, value, near, mid, swap, out, base, bundles):
    rows = query.shape[0]
    block = pl.BlockSpec((rows, WIDE), lambda b, _: (0, base + b))
    pair = pl.BlockSpec((2, rows, WIDE), lambda b, _: (0, 0, b))
    pairs = rows * (3 * rows + SUB) * BUNDLE * bundles
    filled = [] if out is None else [out]
    return pl.pallas_call(
        attend_kernel,
        grid_spec=pltpu.PrefetchScalarGridSpec(
            num_scalar_prefetch=1,
            grid=(bundles,),
            in_specs=[block, block, block, pair, pair, pair]
            + [pl.BlockSpec(memory_space=pl.ANY)] * len(filled),
            out_specs=block,
        ),
        out_shape=jax.ShapeDtypeStruct(query.shape, query.dtype),
        input_output_aliases={7: 0} if filled else {},
        compiler_params=pltpu.CompilerParams(vmem_limit_bytes=VMEM_BYTES),
        cost_estimate=pl.CostEstimate(
            flops=2 * pairs * 512,
            bytes_accessed=20 * rows * bundles * WIDE,
            transcendentals=pairs,
        ),
        name="attend",
    )(info, query, key, value, near, mid, swap, *filled)


def state_kernel(key_ref, value_ref, decay_ref, exact_ref, sent_ref):
    lane = lax.broadcasted_iota(jnp.int32, (DH, LANES), 1)
    for head in range(BUNDLE):
        lanes = slice(head * DH, (head + 1) * DH)
        running = decay_ref[0, :, head : head + 1]
        final = running[-1:, :]
        key = key_ref[:, lanes].astype(jnp.float32) * jnp.exp(final - running)
        state = lax.dot_general(
            key.astype(jnp.bfloat16),
            value_ref[:, lanes],
            (((0,), (0,)), ((), ())),
            preferred_element_type=jnp.float32,
        )
        state = jnp.concatenate([state, jnp.zeros((DH, LANES - DH), jnp.float32)], axis=1)
        exact = jnp.where(lane == DH, final, state)
        exact_ref[head] = exact
        coarse = exact.astype(jnp.bfloat16).astype(jnp.float32)
        rest = (final - final.astype(jnp.bfloat16).astype(jnp.float32))
        sent_ref[head] = jnp.where(lane == DH + 1, rest, coarse).astype(jnp.bfloat16)


def local_state(key, value, decay_cols):
    rows, width = key.shape
    bundles = width // WIDE
    block = pl.BlockSpec((rows, WIDE), lambda b: (0, b))
    out = pl.BlockSpec((BUNDLE, DH, LANES), lambda b: (b, 0, 0))
    heads = bundles * BUNDLE
    return pl.pallas_call(
        state_kernel,
        grid=(bundles,),
        in_specs=[block, block, pl.BlockSpec((1, rows, BUNDLE), lambda b: (b, 0, 0))],
        out_specs=[out, out],
        out_shape=[
            jax.ShapeDtypeStruct((heads, DH, LANES), jnp.float32),
            jax.ShapeDtypeStruct((heads, DH, LANES), jnp.bfloat16),
        ],
        compiler_params=pltpu.CompilerParams(vmem_limit_bytes=VMEM_BYTES),
        cost_estimate=pl.CostEstimate(
            flops=2 * rows * heads * 256 * 256, bytes_accessed=4 * rows * width, transcendentals=0
        ),
        name="local_state",
    )(key, value, decay_cols)


def opened(message):
    wide = message.astype(jnp.float32)
    lane = lax.broadcasted_iota(jnp.int32, wide.shape, 2)
    return jnp.where(lane == DH, wide + wide[:, :, DH + 1 :][:, :, :1], wide)


def closed(exact):
    lane = lax.broadcasted_iota(jnp.int32, exact.shape, 2)
    decay = exact[:, :, DH : DH + 1]
    rest = decay - lax.reduce_precision(decay, 8, 7)
    return jnp.where(lane == DH + 1, rest, exact).astype(jnp.bfloat16)


def joined(earlier, later):
    lane = lax.broadcasted_iota(jnp.int32, earlier.shape, 2)
    kept = jnp.exp(later[:, :, DH : DH + 1])
    return jnp.where(lane == DH, earlier + later, earlier * kept + later)


def mix_kernel(query_ref, key_ref, value_ref, col_ref, row_ref, state_ref, out_ref):
    rows = query_ref.shape[0]
    parts = rows // SUB
    row = lax.broadcasted_iota(jnp.int32, (SUB, SUB), 0)
    col = lax.broadcasted_iota(jnp.int32, (SUB, SUB), 1)
    causal = col <= row
    for part in range(parts):
        first = part * SUB
        here = slice(first, first + SUB)
        outs = []
        for head in range(BUNDLE):
            lanes = slice(head * DH, (head + 1) * DH)
            query = query_ref[here, lanes]
            down = col_ref[0, here, head : head + 1]
            state = state_ref[head][:, :DH].astype(jnp.bfloat16)
            scaled = (query.astype(jnp.float32) * jnp.exp(down)).astype(jnp.bfloat16)
            result = jnp.dot(scaled, state, preferred_element_type=jnp.float32)
            for other in range(part + 1):
                there = slice(other * SUB, (other + 1) * SUB)
                score = lax.dot_general(
                    query,
                    key_ref[there, lanes],
                    (((1,), (1,)), ((), ())),
                    preferred_element_type=jnp.float32,
                )
                gap = down - row_ref[0, head : head + 1, there]
                if other == part:
                    gap = jnp.where(causal, gap, -jnp.inf)
                mixing = (score * jnp.exp(gap)).astype(jnp.bfloat16)
                result = result + jnp.dot(
                    mixing, value_ref[there, lanes], preferred_element_type=jnp.float32
                )
            square = jnp.mean(result * result, axis=1, keepdims=True)
            outs.append(result * lax.rsqrt(square + EPS_NORM))
        out_ref[here, :] = jnp.concatenate(outs, axis=1).astype(out_ref.dtype)


def mixed(query, key, value, decay_cols, decay_rows, state):
    rows, width = query.shape
    bundles = width // WIDE
    heads = bundles * BUNDLE
    block = pl.BlockSpec((rows, WIDE), lambda b: (0, b))
    return pl.pallas_call(
        mix_kernel,
        grid=(bundles,),
        in_specs=[
            block,
            block,
            block,
            pl.BlockSpec((1, rows, BUNDLE), lambda b: (b, 0, 0)),
            pl.BlockSpec((1, BUNDLE, rows), lambda b: (b, 0, 0)),
            pl.BlockSpec((BUNDLE, DH, LANES), lambda b: (b, 0, 0)),
        ],
        out_specs=block,
        out_shape=jax.ShapeDtypeStruct((rows, width), jnp.bfloat16),
        compiler_params=pltpu.CompilerParams(vmem_limit_bytes=VMEM_BYTES),
        cost_estimate=pl.CostEstimate(
            flops=2 * heads * rows * rows * 512,
            bytes_accessed=8 * rows * width,
            transcendentals=heads * rows * rows,
        ),
        name="mixed",
    )(query, key, value, decay_cols, decay_rows, state)


def group_sizes(bundles):
    if bundles >= 8:
        return [2] * (bundles // 2 - 1) + [1, 1]
    return [1] * bundles


def per_device(query1, key1, value1, log_decay, out_weight, query2, key2, value2):
    rows, width = query1.shape
    heads = log_decay.shape[1]
    bundles = heads // BUNDLE
    half = heads // 2
    count = lax.axis_size("ctx")
    position = lax.axis_index("ctx")
    core = lax.rem(position, 2)
    info = jnp.full((1,), position, jnp.int32)

    def moved(value, pairs):
        return lax.ppermute(value, "ctx", [(s, t) for s, t in pairs if 0 <= t < count])

    everyone = range(count)
    step_pairs = [(s, s + 3 if s % 2 else s + 1) for s in everyone]
    chip_pairs = [(s, s + 2) for s in everyone if s % 4 != 3]
    back_pairs = [(s, s - 1) for s in everyone if s % 4 == 2 and s > 2]
    swap_pairs = [(s, s ^ 1) for s in everyone]

    sizes = group_sizes(bundles)
    bases = [sum(sizes[:g]) for g in range(len(sizes))]
    near, chip = {}, {}

    def begin(group, deps):
        sent = pack(key2, value2, bases[group], sizes[group], deps)
        near[group] = moved(sent, step_pairs)
        chip[group] = moved(sent, chip_pairs)

    begin(0, [])
    if len(sizes) > 1:
        begin(1, [])

    running = jnp.cumsum(log_decay, axis=0)
    decay_cols = running.reshape(rows, bundles, BUNDLE).transpose(1, 0, 2)
    decay_rows = running.T.reshape(bundles, BUNDLE, rows)
    exact, sent = local_state(key1, value1, decay_cols)
    other = opened(moved(sent, swap_pairs))
    earlier = jnp.where(core == 0, exact, other)
    later = jnp.where(core == 0, other, exact)
    chip_state = lax.dynamic_slice_in_dim(joined(earlier, later), core * half, half, 0)
    before = jnp.zeros_like(chip_state)
    distance = 1
    while distance < count // 2:
        arrived = opened(
            moved(closed(chip_state), [(s, s + 2 * distance) for s in everyone])
        )
        before = joined(arrived, before)
        chip_state = joined(arrived, chip_state)
        distance *= 2
    other_half = opened(moved(closed(before), swap_pairs))
    before = jnp.where(
        core == 0,
        jnp.concatenate([before, other_half], axis=0),
        jnp.concatenate([other_half, before], axis=0),
    )
    incoming = jnp.where(core == 0, before, joined(before, earlier))
    normed = mixed(query1, key1, value1, decay_cols, decay_rows, incoming)
    linear_mixed = lax.psum_scatter(
        jnp.dot(normed, out_weight, preferred_element_type=jnp.float32).astype(jnp.bfloat16),
        "head",
        scatter_dimension=0,
        tiled=True,
    )

    attended = None
    for group in range(len(sizes)):
        back = moved(near[group], back_pairs)
        mid = jnp.where(lax.rem(position, 4) == 1, back, chip[group])
        swap = moved(mid, swap_pairs)
        if group + 2 < len(sizes):
            begin(group + 2, [chip[group]])
        attended = attend(
            info, query2, key2, value2, near[group], mid, swap, attended, bases[group], sizes[group]
        )
    return (linear_mixed, attended)


def solution(mesh):
    in_specs = (
        P("ctx", "head"),
        P("ctx", "head"),
        P("ctx", "head"),
        P("ctx", "head"),
        P("head", None),
        P("ctx", "head"),
        P("ctx", "head"),
        P("ctx", "head"),
    )
    out_specs = (P(("ctx", "head"), None), P("ctx", "head"))
    return jax.shard_map(
        per_device, mesh=mesh, in_specs=in_specs, out_specs=out_specs, check_vma=False
    )
```

```python
import functools
import math

import jax
import jax.numpy as jnp
from jax import lax
from jax.experimental import pallas as pl
from jax.experimental.pallas import tpu as pltpu
from jax.sharding import PartitionSpec as P

DH = 96
SUB = 256
BUNDLE = 4
WIDE = BUNDLE * DH
LANES = 128
EPS_NORM = 1e-06
VMEM_BYTES = 60 * 1024 * 1024
WINDOWS = ((0, 128, 0), (0, 256, 96), (128, 256, 64), (256, 128, 32))


def cheap():
    return pl.CostEstimate(flops=1000, bytes_accessed=1000, transcendentals=0)


def params():
    return pltpu.CompilerParams(vmem_limit_bytes=VMEM_BYTES)


def untouched(deps):
    return [pl.BlockSpec(memory_space=pltpu.HBM)] * len(deps)


def gate_kernel(*refs):
    del refs


def gate(value, deps):
    return pl.pallas_call(
        gate_kernel,
        in_specs=untouched([value, *deps]),
        out_specs=pl.BlockSpec(memory_space=pltpu.HBM),
        out_shape=jax.ShapeDtypeStruct(value.shape, value.dtype),
        input_output_aliases={0: 0},
        compiler_params=params(),
        cost_estimate=cheap(),
        name="gate",
    )(value, *deps)


def head_lanes(shape, start):
    lane = lax.broadcasted_iota(jnp.int32, shape, len(shape) - 1)
    return (lane >= start) & (lane < start + DH)


def pack_kernel(key_ref, value_ref, *rest):
    out_ref = rest[-1]
    out_ref[0] = key_ref[...]
    out_ref[1] = value_ref[...]


def pack(key, value, base, bundles, deps):
    rows = key.shape[0]
    block = pl.BlockSpec((rows, WIDE), lambda b: (0, base + b))
    return pl.pallas_call(
        pack_kernel,
        grid=(bundles,),
        in_specs=[block, block] + untouched(deps),
        out_specs=pl.BlockSpec((2, rows, WIDE), lambda b: (0, 0, b)),
        out_shape=jax.ShapeDtypeStruct((2, rows, bundles * WIDE), key.dtype),
        compiler_params=params(),
        cost_estimate=cheap(),
        name="pack",
    )(key, value, *deps)


def pick_kernel(info, chip_ref, back_ref, *rest):
    out_ref = rest[-1]
    from_back = lax.rem(info[0], 4) == 1

    @pl.when(from_back)
    def _():
        out_ref[...] = back_ref[...]

    @pl.when(jnp.logical_not(from_back))
    def _():
        out_ref[...] = chip_ref[...]


def pick(info, chip, back, deps):
    _, rows, width = chip.shape
    shape = (2, rows, WIDE)

    def from_chip(b, info):
        return (0, 0, jnp.where(lax.rem(info[0], 4) == 1, 0, b))

    def from_back(b, info):
        return (0, 0, jnp.where(lax.rem(info[0], 4) == 1, b, 0))

    return pl.pallas_call(
        pick_kernel,
        grid_spec=pltpu.PrefetchScalarGridSpec(
            num_scalar_prefetch=1,
            grid=(width // WIDE,),
            in_specs=[pl.BlockSpec(shape, from_chip), pl.BlockSpec(shape, from_back)]
            + untouched(deps),
            out_specs=pl.BlockSpec(shape, lambda b, _: (0, 0, b)),
        ),
        out_shape=jax.ShapeDtypeStruct(chip.shape, chip.dtype),
        compiler_params=params(),
        cost_estimate=cheap(),
        name="pick",
    )(info, chip, back, *deps)


def attend_body(exists, query_ref, slots, out_ref):
    rows = query_ref.shape[0]
    scale = math.log2(math.e) / math.sqrt(DH)
    row = lax.broadcasted_iota(jnp.int32, (SUB, SUB), 0)
    col = lax.broadcasted_iota(jnp.int32, (SUB, SUB), 1)
    newer, older = col > row, col <= row
    low = jnp.float32(-1e30)
    units = [(part, window) for part in range(rows // SUB) for window in WINDOWS]

    def spans(part):
        first = part * SUB
        return [(first, rows), (0, rows), (0, rows), (0, first + SUB)]

    def score_unit(part, window):
        start, width, place = window
        lanes = slice(start, start + width)
        query = query_ref[part * SUB : (part + 1) * SUB, lanes]
        query = jnp.where(head_lanes(query.shape, place), query, jnp.zeros_like(query))
        tiles, peak = [], None
        for slot in range(4):
            begin, end = spans(part)[slot]
            tiles.append([])
            top = None
            for at in range(begin, end, SUB):
                score = lax.dot_general(
                    query,
                    slots[slot][0][at : at + SUB, lanes],
                    (((1,), (1,)), ((), ())),
                    preferred_element_type=jnp.float32,
                )
                if slot == 0 and at == begin:
                    score = jnp.where(newer, score, low)
                if slot == 3 and at == end - SUB:
                    score = jnp.where(older, score, low)
                tiles[slot].append(score)
                for lane in range(0, SUB, LANES):
                    piece = score[:, lane : lane + LANES]
                    top = piece if top is None else jnp.maximum(top, piece)
            if slot < 3:
                top = jnp.where(exists[slot], top, low)
            peak = top if peak is None else jnp.maximum(peak, top)
        return tiles, jnp.max(peak, axis=1, keepdims=True) * scale

    def value_unit(part, window, tiles, peak):
        start, width, place = window
        lanes = slice(start, start + width)
        result = None
        for slot in range(4):
            begin, end = spans(part)[slot]
            shift = peak
            if slot < 3:
                shift = jnp.where(exists[slot], peak, jnp.float32(1e30))
            for index, at in enumerate(range(begin, end, SUB)):
                weight = jnp.exp2(tiles[slot][index] * scale - shift).astype(jnp.bfloat16)
                value = slots[slot][1][at : at + SUB, lanes]
                value = jnp.where(head_lanes(value.shape, place), value, jnp.ones_like(value))
                term = jnp.dot(weight, value, preferred_element_type=jnp.float32)
                result = term if result is None else result + term
        spare = 96 if place == 0 else 0
        result = result * (1.0 / result[:, spare : spare + 1])
        return jnp.where(head_lanes(result.shape, place), result, 0.0)

    ready = score_unit(*units[0])
    tiles_out = [None] * (WIDE // LANES)
    for index, (part, window) in enumerate(units):
        following = score_unit(*units[index + 1]) if index + 1 < len(units) else None
        result = value_unit(part, window, *ready)
        for lane in range(0, window[1], LANES):
            place = (window[0] + lane) // LANES
            piece = result[:, lane : lane + LANES]
            tiles_out[place] = piece if tiles_out[place] is None else tiles_out[place] + piece
        if window is WINDOWS[-1]:
            for place, piece in enumerate(tiles_out):
                out_ref[
                    part * SUB : (part + 1) * SUB, place * LANES : (place + 1) * LANES
                ] = piece.astype(out_ref.dtype)
            tiles_out = [None] * (WIDE // LANES)
        ready = following


def attend_kernel(info, query_ref, key_ref, value_ref, near_ref, mid_ref, swap_ref, *rest):
    out_ref = rest[-1]
    position = info[0]
    exists = [position >= 3, position >= 2, position >= 1]
    own = (key_ref, value_ref)
    near, mid, swap = [(r.at[0], r.at[1]) for r in (near_ref, mid_ref, swap_ref)]
    core = lax.rem(position, 2)

    @pl.when(core == 0)
    def _():
        attend_body(exists, query_ref, [near, mid, swap, own], out_ref)

    @pl.when(core == 1)
    def _():
        attend_body(exists, query_ref, [swap, mid, near, own], out_ref)


def attend(info, query, key, value, near, mid, swap, out, base, deps):
    rows = query.shape[0]
    block = pl.BlockSpec((rows, WIDE), lambda b, _: (0, base + b))
    pair = pl.BlockSpec((2, rows, WIDE), lambda b, _: (0, 0, b))
    filled = [] if out is None else [out]
    return pl.pallas_call(
        attend_kernel,
        grid_spec=pltpu.PrefetchScalarGridSpec(
            num_scalar_prefetch=1,
            grid=(near.shape[2] // WIDE,),
            in_specs=[block, block, block, pair, pair, pair] + untouched([*filled, *deps]),
            out_specs=block,
        ),
        out_shape=jax.ShapeDtypeStruct(query.shape, query.dtype),
        input_output_aliases={7: 0} if filled else {},
        compiler_params=params(),
        cost_estimate=cheap(),
        name="attend",
    )(info, query, key, value, near, mid, swap, *filled, *deps)


def opened(message):
    wide = message.astype(jnp.float32)
    lane = lax.broadcasted_iota(jnp.int32, wide.shape, wide.ndim - 1)
    return jnp.where(lane == DH, wide + wide[..., DH + 1 : DH + 2], wide)


def closed(exact):
    lane = lax.broadcasted_iota(jnp.int32, exact.shape, exact.ndim - 1)
    decay = exact[..., DH : DH + 1]
    rest = decay - decay.astype(jnp.bfloat16).astype(jnp.float32)
    return jnp.where(lane == DH + 1, rest, exact).astype(jnp.bfloat16)


def joined(earlier, later):
    lane = lax.broadcasted_iota(jnp.int32, earlier.shape, earlier.ndim - 1)
    kept = jnp.exp(later[..., DH : DH + 1])
    return jnp.where(lane == DH, earlier + later, earlier * kept + later)


def state_kernel(key_ref, value_ref, decay_ref, *rest):
    exact_ref, first_ref, sent_ref = rest[-3:]
    rows = key_ref.shape[0]
    lane = lax.broadcasted_iota(jnp.int32, (DH, LANES), 1)
    key_t = key_ref[...].T
    for head, (start, width, place) in enumerate(WINDOWS):
        lanes = slice(start, start + width)
        state, before = None, None
        for at in range(0, rows, SUB):
            running = decay_ref[0, at : at + SUB, head : head + 1]
            anchor = running[SUB - 1 :, :]
            value = value_ref[at : at + SUB, lanes].astype(jnp.float32) * jnp.exp(anchor - running)
            update = jnp.dot(
                key_t[head * DH : (head + 1) * DH, at : at + SUB],
                value.astype(jnp.bfloat16),
                preferred_element_type=jnp.float32,
            )
            if at + SUB == rows:
                first_ref[head] = narrow(state, place)
            state = update if state is None else state * jnp.exp(anchor - before) + update
            before = anchor
        exact = jnp.where(lane == DH, before, narrow(state, place))
        exact_ref[head] = exact
        sent_ref[head] = closed(exact)


def narrow(state, place):
    width = state.shape[1]
    if place:
        state = pltpu.roll(state, width - place, axis=1)
    state = state[:, :LANES]
    lane = lax.broadcasted_iota(jnp.int32, state.shape, 1)
    return jnp.where(lane < DH, state, 0.0)


def widen(state, width, place):
    lane = lax.broadcasted_iota(jnp.int32, state.shape, 1)
    state = jnp.where(lane < DH, state, 0.0)
    if width > LANES:
        state = jnp.concatenate([state, jnp.zeros((DH, width - LANES), jnp.float32)], axis=1)
    if place:
        state = pltpu.roll(state, place, axis=1)
    pads = []
    if place:
        pads.append(jnp.zeros((place, width), jnp.float32))
    pads.append(state)
    if place + DH < width:
        pads.append(jnp.zeros((width - place - DH, width), jnp.float32))
    return jnp.concatenate(pads, axis=0).astype(jnp.bfloat16)


def local_state(key, value, decay_cols, deps):
    rows, width = key.shape
    bundles = width // WIDE
    block = pl.BlockSpec((rows, WIDE), lambda b: (0, b))
    out = pl.BlockSpec((BUNDLE, DH, LANES), lambda b: (b, 0, 0))
    shape = (bundles * BUNDLE, DH, LANES)
    return pl.pallas_call(
        state_kernel,
        grid=(bundles,),
        in_specs=[block, block, pl.BlockSpec((1, rows, BUNDLE), lambda b: (b, 0, 0))]
        + untouched(deps),
        out_specs=[out, out, out],
        out_shape=[
            jax.ShapeDtypeStruct(shape, jnp.float32),
            jax.ShapeDtypeStruct(shape, jnp.float32),
            jax.ShapeDtypeStruct(shape, jnp.bfloat16),
        ],
        compiler_params=params(),
        cost_estimate=cheap(),
        name="local_state",
    )(key, value, decay_cols, *deps)


def chip_state_kernel(info, exact_ref, other_ref, *rest):
    chip_ref, sent_ref = rest[-2:]
    even = lax.rem(info[0], 2) == 0
    mine, other = exact_ref[...], opened(other_ref[...])
    chip = joined(jnp.where(even, mine, other), jnp.where(even, other, mine))
    chip_ref[...] = chip
    sent_ref[...] = closed(chip)


def chip_state(info, exact, other, deps):
    half = exact.shape[0] // 2
    shape = (half, DH, LANES)
    block = pl.BlockSpec((BUNDLE, DH, LANES), lambda b, _: (b, 0, 0))
    steps = half // BUNDLE

    def mine(b, info):
        return (lax.rem(info[0], 2) * steps + b, 0, 0)

    return pl.pallas_call(
        chip_state_kernel,
        grid_spec=pltpu.PrefetchScalarGridSpec(
            num_scalar_prefetch=1,
            grid=(steps,),
            in_specs=[pl.BlockSpec((BUNDLE, DH, LANES), mine)] * 2 + untouched(deps),
            out_specs=[block, block],
        ),
        out_shape=[
            jax.ShapeDtypeStruct(shape, jnp.float32),
            jax.ShapeDtypeStruct(shape, jnp.bfloat16),
        ],
        compiler_params=params(),
        cost_estimate=cheap(),
        name="chip_state",
    )(info, exact, other, *deps)


def join_kernel(start, last, chip_ref, before_ref, arrived_ref, *rest):
    chip_out, before_out, sent_ref = rest[-3:]
    arrived = opened(arrived_ref[...])
    before = arrived if start else joined(arrived, before_ref[...])
    before_out[...] = before
    if last:
        sent_ref[...] = closed(before)
    else:
        chip = joined(arrived, chip_ref[...])
        chip_out[...] = chip
        sent_ref[...] = closed(chip)


def join(chip, before, arrived, start, last, deps):
    block = pl.BlockSpec((BUNDLE, DH, LANES), lambda b: (b, 0, 0))
    return pl.pallas_call(
        functools.partial(join_kernel, start, last),
        grid=(chip.shape[0] // BUNDLE,),
        in_specs=[block] * 3 + untouched(deps),
        out_specs=[block] * 3,
        out_shape=[
            jax.ShapeDtypeStruct(chip.shape, jnp.float32),
            jax.ShapeDtypeStruct(chip.shape, jnp.float32),
            jax.ShapeDtypeStruct(chip.shape, jnp.bfloat16),
        ],
        compiler_params=params(),
        cost_estimate=cheap(),
        name="join",
    )(chip, before, arrived, *deps)


def spread(result, start, tiles_out):
    for lane in range(0, result.shape[1], LANES):
        tile = (start + lane) // LANES
        piece = result[:, lane : lane + LANES]
        tiles_out[tile] = piece if tiles_out[tile] is None else tiles_out[tile] + piece


def mix_local_kernel(query_ref, key_ref, value_ref, col_ref, row_ref, first_ref, *rest):
    out_ref = rest[-1]
    rows = query_ref.shape[0]
    row = lax.broadcasted_iota(jnp.int32, (SUB, SUB), 0)
    col = lax.broadcasted_iota(jnp.int32, (SUB, SUB), 1)
    causal = col <= row
    for at in range(0, rows, SUB):
        here = slice(at, at + SUB)
        tiles_out = [None] * (WIDE // LANES)
        for head, (start, width, place) in enumerate(WINDOWS):
            lanes = slice(start, start + width)
            query = query_ref[here, lanes]
            query = jnp.where(head_lanes(query.shape, place), query, jnp.zeros_like(query))
            down = col_ref[0, here, head : head + 1]
            score = lax.dot_general(
                query,
                key_ref[here, lanes],
                (((1,), (1,)), ((), ())),
                preferred_element_type=jnp.float32,
            )
            gap = jnp.where(causal, down - row_ref[0, head : head + 1, here], -jnp.inf)
            mixing = (score * jnp.exp(gap)).astype(jnp.bfloat16)
            result = jnp.dot(mixing, value_ref[here, lanes], preferred_element_type=jnp.float32)
            if at:
                since = down - col_ref[0, at - 1 : at, head : head + 1]
                scaled = (query.astype(jnp.float32) * jnp.exp(since)).astype(jnp.bfloat16)
                result = result + jnp.dot(
                    scaled, widen(first_ref[head], width, place), preferred_element_type=jnp.float32
                )
            spread(jnp.where(head_lanes(result.shape, place), result, 0.0), start, tiles_out)
        for tile, piece in enumerate(tiles_out):
            out_ref[here, tile * LANES : (tile + 1) * LANES] = piece


def mix_local(query, key, value, decay_cols, decay_rows, first, deps):
    rows, width = query.shape
    block = pl.BlockSpec((rows, WIDE), lambda b: (0, b))
    return pl.pallas_call(
        mix_local_kernel,
        grid=(width // WIDE,),
        in_specs=[
            block,
            block,
            block,
            pl.BlockSpec((1, rows, BUNDLE), lambda b: (b, 0, 0)),
            pl.BlockSpec((1, BUNDLE, rows), lambda b: (b, 0, 0)),
            pl.BlockSpec((BUNDLE, DH, LANES), lambda b: (b, 0, 0)),
        ]
        + untouched(deps),
        out_specs=block,
        out_shape=jax.ShapeDtypeStruct((rows, width), jnp.float32),
        compiler_params=params(),
        cost_estimate=cheap(),
        name="mix_local",
    )(query, key, value, decay_cols, decay_rows, first, *deps)


def mix_final_kernel(half, info, query_ref, local_ref, col_ref, own_ref, sent_ref, other_ref, *rest):
    out_ref = rest[-1]
    rows = query_ref.shape[0]
    core = lax.rem(info[0], 2)
    mine = (pl.program_id(0) >= half).astype(jnp.int32) == core
    states = []
    for head, (_, width, place) in enumerate(WINDOWS):
        state = jnp.where(mine, own_ref[head], opened(sent_ref[head]))
        state = jnp.where(core == 0, state, joined(state, opened(other_ref[head])))
        states.append(widen(state, width, place))
    for at in range(0, rows, SUB):
        here = slice(at, at + SUB)
        tiles_out = [None] * (WIDE // LANES)
        for head, (start, width, place) in enumerate(WINDOWS):
            lanes = slice(start, start + width)
            inside = head_lanes((SUB, width), place)
            query = jnp.where(inside, query_ref[here, lanes].astype(jnp.float32), 0.0)
            scaled = (query * jnp.exp(col_ref[0, here, head : head + 1])).astype(jnp.bfloat16)
            result = jnp.dot(scaled, states[head], preferred_element_type=jnp.float32)
            result = jnp.where(inside, result + local_ref[here, lanes], 0.0)
            square = jnp.sum(result * result, axis=1, keepdims=True) * (1.0 / DH)
            spread(result * lax.rsqrt(square + EPS_NORM), start, tiles_out)
        for tile, piece in enumerate(tiles_out):
            out_ref[here, tile * LANES : (tile + 1) * LANES] = piece.astype(out_ref.dtype)


def mix_final(info, query, local, decay_cols, own, sent, other, deps):
    rows, width = query.shape
    bundles = width // WIDE
    half = bundles // 2
    block = pl.BlockSpec((rows, WIDE), lambda b, _: (0, b))
    states = pl.BlockSpec((BUNDLE, DH, LANES), lambda b, _: (b, 0, 0))
    halves = pl.BlockSpec((BUNDLE, DH, LANES), lambda b, _: (lax.rem(b, half), 0, 0))
    return pl.pallas_call(
        functools.partial(mix_final_kernel, half),
        grid_spec=pltpu.PrefetchScalarGridSpec(
            num_scalar_prefetch=1,
            grid=(bundles,),
            in_specs=[
                block,
                block,
                pl.BlockSpec((1, rows, BUNDLE), lambda b, _: (b, 0, 0)),
                halves,
                halves,
                states,
            ]
            + untouched(deps),
            out_specs=block,
        ),
        out_shape=jax.ShapeDtypeStruct((rows, width), jnp.bfloat16),
        compiler_params=params(),
        cost_estimate=cheap(),
        name="mix_final",
    )(info, query, local, decay_cols, own, sent, other, *deps)


def group_sizes(bundles):
    if bundles == 8:
        return [2, 3, 2, 1]
    return [1] * bundles


def per_device(query1, key1, value1, log_decay, out_weight, query2, key2, value2):
    rows, width = query1.shape
    bundles = width // WIDE
    count = lax.axis_size("ctx")
    position = lax.axis_index("ctx")
    info = jnp.full((1,), position, jnp.int32)

    def moved(value, pairs):
        return lax.ppermute(value, "ctx", [(s, t) for s, t in pairs if 0 <= t < count])

    everyone = range(count)
    step_pairs = [(s, s + 3 if s % 2 else s + 1) for s in everyone]
    chip_pairs = [(s, s + 2) for s in everyone if s % 4 != 3]
    back_pairs = [(s, s - 1) for s in everyone if s % 4 == 2 and s > 2]
    swap_pairs = [(s, s ^ 1) for s in everyone]

    sizes = group_sizes(bundles)
    groups = len(sizes)
    bases = [sum(sizes[:g]) for g in range(groups)]
    near, chip, back, mid, swap = {}, {}, {}, {}, {}
    done = {"last": [], "attended": None}

    def do_pack(group):
        if group < groups:
            sent = pack(key2, value2, bases[group], sizes[group], done["last"])
            near[group] = moved(sent, step_pairs)
            chip[group] = moved(sent, chip_pairs)
            done["last"] = [sent]

    def do_back(group):
        if group < groups:
            near[group] = gate(near[group], done["last"])
            back[group] = moved(near[group], back_pairs)

    def do_pick(group):
        if group < groups:
            mid[group] = pick(info, chip[group], back[group], done["last"])
            swap[group] = moved(mid[group], swap_pairs)
            done["last"] = [mid[group]]

    def do_attend(group):
        if group < groups:
            done["attended"] = attend(
                info, query2, key2, value2, near[group], mid[group], swap[group],
                done["attended"], bases[group], done["last"],
            )
            done["last"] = [done["attended"]]

    light = {"distance": 1, "before": None}

    def do_state():
        running = jnp.cumsum(log_decay, axis=0)
        light["cols"] = running.reshape(rows, bundles, BUNDLE).transpose(1, 0, 2)
        light["rows"] = running.T.reshape(bundles, BUNDLE, rows)
        exact, first, sent = local_state(key1, value1, light["cols"], done["last"])
        light["first"] = first
        light["other"] = moved(sent, swap_pairs)
        light["exact"] = exact
        done["last"] = [sent]

    def do_chip():
        light["chip"], sent = chip_state(info, light["exact"], light["other"], done["last"])
        light["arrived"] = moved(sent, [(s, s + 2) for s in everyone])
        light["distance"] = 1
        done["last"] = [sent]

    def do_join():
        if light["distance"] < count // 2:
            start = light["distance"] == 1
            light["distance"] *= 2
            last = light["distance"] >= count // 2
            before = light["chip"] if start else light["before"]
            light["chip"], light["before"], sent = join(
                light["chip"], before, light["arrived"], start, last, done["last"]
            )
            pairs = swap_pairs if last else [(s, s + 2 * light["distance"]) for s in everyone]
            light["arrived"] = moved(sent, pairs)
            done["last"] = [sent]

    def do_mix_local():
        light["local"] = mix_local(
            query1, key1, value1, light["cols"], light["rows"], light["first"], done["last"]
        )
        done["last"] = [light["local"]]

    def do_mix_final():
        while light["distance"] < count // 2:
            do_join()
        light["normed"] = mix_final(
            info, query1, light["local"], light["cols"], light["before"], light["arrived"],
            light["other"], done["last"],
        )
        done["last"] = [light["normed"]]

    def do_project():
        product = jnp.dot(light["normed"], out_weight, preferred_element_type=jnp.float32)
        product = product.astype(jnp.bfloat16)
        done["linear"] = lax.psum_scatter(product, "head", scatter_dimension=0, tiled=True)
        done["last"] = [product]

    def wait_chip(group):
        done["last"] = done["last"] + [chip[group]]

    do_pack(0)
    do_state()
    do_pack(1)
    do_back(0)
    do_mix_local()
    wait_chip(0)
    do_chip()
    do_pick(0)
    do_join()
    do_attend(0)
    do_join()
    do_back(1)
    wait_chip(1)
    do_join()
    do_pack(2)
    do_mix_final()
    do_pick(1)
    do_project()
    do_back(2)
    do_pack(3)
    do_attend(1)
    do_back(3)
    do_pick(2)
    do_pick(3)
    do_attend(2)
    do_attend(3)
    return (done["linear"], done["attended"])


def solution(mesh):
    in_specs = (
        P("ctx", "head"),
        P("ctx", "head"),
        P("ctx", "head"),
        P("ctx", "head"),
        P("head", None),
        P("ctx", "head"),
        P("ctx", "head"),
        P("ctx", "head"),
    )
    out_specs = (P(("ctx", "head"), None), P("ctx", "head"))
    return jax.shard_map(
        per_device, mesh=mesh, in_specs=in_specs, out_specs=out_specs, check_vma=False
    )
```

```python
import functools
import math

import jax
import jax.numpy as jnp
from jax import lax
from jax.experimental import pallas as pl
from jax.experimental.pallas import tpu as pltpu
from jax.sharding import PartitionSpec as P

DH = 96
SUB = 256
BUNDLE = 4
WIDE = BUNDLE * DH
LANES = 128
EPS_NORM = 1e-06
VMEM_BYTES = 63 * 1024 * 1024
WINDOWS = ((0, 128, 0), (0, 256, 96), (128, 256, 64), (256, 128, 32))


def cheap():
    return pl.CostEstimate(flops=1000, bytes_accessed=1000, transcendentals=0)


def params():
    return pltpu.CompilerParams(vmem_limit_bytes=VMEM_BYTES)


def untouched(deps):
    return [pl.BlockSpec(memory_space=pl.ANY)] * len(deps)


def gate_kernel(*refs):
    del refs


def gate(value, deps):
    return pl.pallas_call(
        gate_kernel,
        in_specs=untouched([value, *deps]),
        out_specs=pl.BlockSpec(memory_space=pl.ANY),
        out_shape=jax.ShapeDtypeStruct(value.shape, value.dtype),
        input_output_aliases={0: 0},
        compiler_params=params(),
        cost_estimate=cheap(),
        name="gate",
    )(value, *deps)


def head_lanes(shape, start):
    lane = lax.broadcasted_iota(jnp.int32, shape, len(shape) - 1)
    return (lane >= start) & (lane < start + DH)


def pack_kernel(base, key_ref, value_ref, *rest):
    out_ref, sems = rest[-2:]
    width = out_ref.shape[2]
    copies = [
        pltpu.make_async_copy(ref.at[:, pl.ds(base * WIDE, width)], out_ref.at[i], sems.at[i])
        for i, ref in enumerate((key_ref, value_ref))
    ]
    for copy in copies:
        copy.start()
    for copy in copies:
        copy.wait()


def pack(key, value, base, bundles, deps):
    rows = key.shape[0]
    return pl.pallas_call(
        functools.partial(pack_kernel, base),
        in_specs=untouched([key, value, *deps]),
        out_specs=pl.BlockSpec(memory_space=pl.ANY),
        out_shape=jax.ShapeDtypeStruct((2, rows, bundles * WIDE), key.dtype),
        scratch_shapes=[pltpu.SemaphoreType.DMA((2,))],
        compiler_params=params(),
        cost_estimate=cheap(),
        name="pack",
    )(key, value, *deps)


def pick_kernel(info, chip_ref, back_ref, *rest):
    out_ref, sem = rest[-2:]
    from_back = lax.rem(info[0], 4) == 1

    @pl.when(from_back)
    def _():
        copy = pltpu.make_async_copy(back_ref, out_ref, sem)
        copy.start()
        copy.wait()

    @pl.when(jnp.logical_not(from_back))
    def _():
        copy = pltpu.make_async_copy(chip_ref, out_ref, sem)
        copy.start()
        copy.wait()


def pick(info, chip, back, deps):
    return pl.pallas_call(
        pick_kernel,
        in_specs=[pl.BlockSpec(memory_space=pltpu.SMEM)] + untouched([chip, back, *deps]),
        out_specs=pl.BlockSpec(memory_space=pl.ANY),
        out_shape=jax.ShapeDtypeStruct(chip.shape, chip.dtype),
        scratch_shapes=[pltpu.SemaphoreType.DMA],
        compiler_params=params(),
        cost_estimate=cheap(),
        name="pick",
    )(info, chip, back, *deps)


def attend_body(exists, query_ref, slots, out_ref):
    rows = query_ref.shape[0]
    scale = math.log2(math.e) / math.sqrt(DH)
    row = lax.broadcasted_iota(jnp.int32, (SUB, SUB), 0)
    col = lax.broadcasted_iota(jnp.int32, (SUB, SUB), 1)
    newer, older = col > row, col <= row
    low = jnp.float32(-1e30)
    units = [(part, window) for part in range(rows // SUB) for window in WINDOWS]

    def spans(part):
        first = part * SUB
        return [(first, rows), (0, rows), (0, rows), (0, first + SUB)]

    def score_unit(part, window):
        start, width, place = window
        lanes = slice(start, start + width)
        query = query_ref[part * SUB : (part + 1) * SUB, lanes]
        query = jnp.where(head_lanes(query.shape, place), query, jnp.zeros_like(query))
        tiles, peak = [], None
        for slot in range(4):
            begin, end = spans(part)[slot]
            tiles.append([])
            top = None
            for at in range(begin, end, SUB):
                score = lax.dot_general(
                    query,
                    slots[slot][0][at : at + SUB, lanes],
                    (((1,), (1,)), ((), ())),
                    preferred_element_type=jnp.float32,
                )
                if slot == 0 and at == begin:
                    score = jnp.where(newer, score, low)
                if slot == 3 and at == end - SUB:
                    score = jnp.where(older, score, low)
                tiles[slot].append(score)
                for lane in range(0, SUB, LANES):
                    piece = score[:, lane : lane + LANES]
                    top = piece if top is None else jnp.maximum(top, piece)
            if slot < 3:
                top = jnp.where(exists[slot], top, low)
            peak = top if peak is None else jnp.maximum(peak, top)
        return tiles, jnp.max(peak, axis=1, keepdims=True) * scale

    def value_unit(part, window, tiles, peak):
        start, width, place = window
        lanes = slice(start, start + width)
        result = None
        for slot in range(4):
            begin, end = spans(part)[slot]
            shift = peak
            if slot < 3:
                shift = jnp.where(exists[slot], peak, jnp.float32(1e30))
            for index, at in enumerate(range(begin, end, SUB)):
                weight = jnp.exp2(tiles[slot][index] * scale - shift).astype(jnp.bfloat16)
                value = slots[slot][1][at : at + SUB, lanes]
                value = jnp.where(head_lanes(value.shape, place), value, jnp.ones_like(value))
                term = jnp.dot(weight, value, preferred_element_type=jnp.float32)
                result = term if result is None else result + term
        spare = 96 if place == 0 else 0
        result = result * (1.0 / result[:, spare : spare + 1])
        return jnp.where(head_lanes(result.shape, place), result, 0.0)

    ready = score_unit(*units[0])
    tiles_out = [None] * (WIDE // LANES)
    for index, (part, window) in enumerate(units):
        following = score_unit(*units[index + 1]) if index + 1 < len(units) else None
        result = value_unit(part, window, *ready)
        for lane in range(0, window[1], LANES):
            place = (window[0] + lane) // LANES
            piece = result[:, lane : lane + LANES]
            tiles_out[place] = piece if tiles_out[place] is None else tiles_out[place] + piece
        if window is WINDOWS[-1]:
            for place, piece in enumerate(tiles_out):
                out_ref[
                    part * SUB : (part + 1) * SUB, place * LANES : (place + 1) * LANES
                ] = piece.astype(out_ref.dtype)
            tiles_out = [None] * (WIDE // LANES)
        ready = following


def attend_bounded(exists, query_ref, slots, out_ref):
    rows = query_ref.shape[0]
    scale = jnp.float32(math.log2(math.e) / math.sqrt(DH))
    row = lax.broadcasted_iota(jnp.int32, (SUB, SUB), 0)
    col = lax.broadcasted_iota(jnp.int32, (SUB, SUB), 1)
    newer, older = col > row, col <= row
    low = jnp.float32(-1e30)
    for part in range(rows // SUB):
        first = part * SUB
        spans = [(first, rows), (0, rows), (0, rows), (0, first + SUB)]
        tiles_out = [None] * (WIDE // LANES)
        for start, width, place in WINDOWS:
            lanes = slice(start, start + width)
            query = query_ref[first : first + SUB, lanes]
            query = jnp.where(head_lanes(query.shape, place), query, jnp.zeros_like(query))
            result = None
            for slot in range(4):
                begin, end = spans[slot]
                weights = []
                for at in range(begin, end, SUB):
                    score = lax.dot_general(
                        query,
                        slots[slot][0][at : at + SUB, lanes],
                        (((1,), (1,)), ((), ())),
                        preferred_element_type=jnp.float32,
                    )
                    if slot == 0 and at == begin:
                        score = jnp.where(newer, score, low)
                    if slot == 3 and at == end - SUB:
                        score = jnp.where(older, score, low)
                    weights.append(jnp.exp2(score * scale).astype(jnp.bfloat16))
                weight = weights[0] if len(weights) == 1 else jnp.concatenate(weights, axis=1)
                value = slots[slot][1][begin:end, lanes]
                one = jnp.ones_like(value)
                if slot < 3:
                    one = jnp.full(value.shape, exists[slot].astype(jnp.float32), value.dtype)
                value = jnp.where(head_lanes(value.shape, place), value, one)
                term = jnp.dot(weight, value, preferred_element_type=jnp.float32)
                result = term if result is None else result + term
            spare = 96 if place == 0 else 0
            result = result * (1.0 / result[:, spare : spare + 1])
            spread(jnp.where(head_lanes(result.shape, place), result, 0.0), start, tiles_out)
        for tile, piece in enumerate(tiles_out):
            out_ref[first : first + SUB, tile * LANES : (tile + 1) * LANES] = piece.astype(
                out_ref.dtype
            )


def spread(result, start, tiles_out):
    for lane in range(0, result.shape[1], LANES):
        tile = (start + lane) // LANES
        piece = result[:, lane : lane + LANES]
        tiles_out[tile] = piece if tiles_out[tile] is None else tiles_out[tile] + piece


def attend_kernel(info, query_ref, key_ref, value_ref, near_ref, mid_ref, swap_ref, *rest):
    out_ref = rest[-1]
    position = info[0]
    exists = [position >= 3, position >= 2, position >= 1]
    own = (key_ref, value_ref)
    near, mid, swap = [(r.at[0], r.at[1]) for r in (near_ref, mid_ref, swap_ref)]
    core = lax.rem(position, 2)
    sums = jnp.abs(query_ref[...].astype(jnp.float32))
    most = None
    for start, width, place in WINDOWS:
        part = sums[:, start : start + width]
        part = jnp.sum(jnp.where(head_lanes(part.shape, place), part, 0.0), axis=1, keepdims=True)
        most = part if most is None else jnp.maximum(most, part)
    top = None
    for key, _ in (near, mid, swap, own):
        one = jnp.max(jnp.abs(key[...]), axis=0, keepdims=True)
        top = one if top is None else jnp.maximum(top, one)
    limit = 100.0 * math.sqrt(DH) / math.log2(math.e)
    bounded = jnp.max(most) * jnp.max(top.astype(jnp.float32)) < limit

    for side in range(2):
        for body, chosen in ((attend_bounded, bounded), (attend_body, jnp.logical_not(bounded))):
            @pl.when((core == side) & chosen)
            def _(body=body, side=side):
                old, new = (near, swap) if side == 0 else (swap, near)
                body(exists, query_ref, [old, mid, new, own], out_ref)


def attend(info, query, key, value, near, mid, swap, out, base, deps):
    rows = query.shape[0]
    block = pl.BlockSpec((rows, WIDE), lambda b, _: (0, base + b))
    pair = pl.BlockSpec((2, rows, WIDE), lambda b, _: (0, 0, b))
    filled = [] if out is None else [out]
    return pl.pallas_call(
        attend_kernel,
        grid_spec=pltpu.PrefetchScalarGridSpec(
            num_scalar_prefetch=1,
            grid=(near.shape[2] // WIDE,),
            in_specs=[block, block, block, pair, pair, pair] + untouched([*filled, *deps]),
            out_specs=block,
        ),
        out_shape=jax.ShapeDtypeStruct(query.shape, query.dtype),
        input_output_aliases={7: 0} if filled else {},
        compiler_params=params(),
        cost_estimate=cheap(),
        name="attend",
    )(info, query, key, value, near, mid, swap, *filled, *deps)


def opened(message):
    wide = message.astype(jnp.float32)
    lane = lax.broadcasted_iota(jnp.int32, wide.shape, wide.ndim - 1)
    return jnp.where(lane == DH, wide + wide[..., DH + 1 : DH + 2], wide)


def closed(exact):
    lane = lax.broadcasted_iota(jnp.int32, exact.shape, exact.ndim - 1)
    decay = exact[..., DH : DH + 1]
    rest = decay - decay.astype(jnp.bfloat16).astype(jnp.float32)
    return jnp.where(lane == DH + 1, rest, exact).astype(jnp.bfloat16)


def joined(earlier, later):
    lane = lax.broadcasted_iota(jnp.int32, earlier.shape, earlier.ndim - 1)
    kept = jnp.exp(later[..., DH : DH + 1])
    return jnp.where(lane == DH, earlier + later, earlier * kept + later)


def state_kernel(key_ref, value_ref, decay_ref, *rest):
    exact_ref, first_ref, sent_ref = rest[-3:]
    rows = key_ref.shape[0]
    lane = lax.broadcasted_iota(jnp.int32, (DH, LANES), 1)
    key_t = key_ref[...].T
    for head, (start, width, place) in enumerate(WINDOWS):
        lanes = slice(start, start + width)
        state, before = None, None
        for at in range(0, rows, SUB):
            running = decay_ref[0, head : head + 1, at : at + SUB]
            anchor = running[:, SUB - 1 :]
            key = key_t[head * DH : (head + 1) * DH, at : at + SUB].astype(jnp.float32)
            update = jnp.dot(
                (key * jnp.exp(anchor - running)).astype(jnp.bfloat16),
                value_ref[at : at + SUB, lanes],
                preferred_element_type=jnp.float32,
            )
            if at + SUB == rows:
                first_ref[head] = narrow(state, place)
            state = update if state is None else state * jnp.exp(anchor - before) + update
            before = anchor
        exact = jnp.where(lane == DH, before, narrow(state, place))
        exact_ref[head] = exact
        sent_ref[head] = closed(exact)


def narrow(state, place):
    width = state.shape[1]
    if place:
        state = pltpu.roll(state, width - place, axis=1)
    state = state[:, :LANES]
    lane = lax.broadcasted_iota(jnp.int32, state.shape, 1)
    return jnp.where(lane < DH, state, 0.0)


def widen(state, width, place):
    lane = lax.broadcasted_iota(jnp.int32, state.shape, 1)
    state = jnp.where(lane < DH, state, 0.0)
    if width > LANES:
        state = jnp.concatenate([state, jnp.zeros((DH, width - LANES), jnp.float32)], axis=1)
    if place:
        state = pltpu.roll(state, place, axis=1)
    pads = []
    if place:
        pads.append(jnp.zeros((place, width), jnp.float32))
    pads.append(state)
    if place + DH < width:
        pads.append(jnp.zeros((width - place - DH, width), jnp.float32))
    return jnp.concatenate(pads, axis=0).astype(jnp.bfloat16)


def local_state(key, value, decay_rows, deps):
    rows, width = key.shape
    bundles = width // WIDE
    block = pl.BlockSpec((rows, WIDE), lambda b: (0, b))
    out = pl.BlockSpec((BUNDLE, DH, LANES), lambda b: (b, 0, 0))
    shape = (bundles * BUNDLE, DH, LANES)
    return pl.pallas_call(
        state_kernel,
        grid=(bundles,),
        in_specs=[block, block, pl.BlockSpec((1, BUNDLE, rows), lambda b: (b, 0, 0))]
        + untouched(deps),
        out_specs=[out, out, out],
        out_shape=[
            jax.ShapeDtypeStruct(shape, jnp.float32),
            jax.ShapeDtypeStruct(shape, jnp.float32),
            jax.ShapeDtypeStruct(shape, jnp.bfloat16),
        ],
        compiler_params=params(),
        cost_estimate=cheap(),
        name="local_state",
    )(key, value, decay_rows, *deps)


def chip_state_kernel(info, exact_ref, other_ref, *rest):
    chip_ref, sent_ref = rest[-2:]
    even = lax.rem(info[0], 2) == 0
    mine, other = exact_ref[...], opened(other_ref[...])
    chip = joined(jnp.where(even, mine, other), jnp.where(even, other, mine))
    chip_ref[...] = chip
    sent_ref[...] = closed(chip)


def chip_state(info, exact, other, deps):
    half = exact.shape[0] // 2
    shape = (half, DH, LANES)
    block = pl.BlockSpec(shape, lambda b, _: (0, 0, 0))

    def mine(b, info):
        return (lax.rem(info[0], 2), 0, 0)

    return pl.pallas_call(
        chip_state_kernel,
        grid_spec=pltpu.PrefetchScalarGridSpec(
            num_scalar_prefetch=1,
            grid=(1,),
            in_specs=[pl.BlockSpec(shape, mine)] * 2 + untouched(deps),
            out_specs=[block, block],
        ),
        out_shape=[
            jax.ShapeDtypeStruct(shape, jnp.float32),
            jax.ShapeDtypeStruct(shape, jnp.bfloat16),
        ],
        compiler_params=params(),
        cost_estimate=cheap(),
        name="chip_state",
    )(info, exact, other, *deps)


def join_kernel(start, last, chip_ref, before_ref, arrived_ref, *rest):
    chip_out, before_out, sent_ref = rest[-3:]
    arrived = opened(arrived_ref[...])
    before = arrived if start else joined(arrived, before_ref[...])
    before_out[...] = before
    if last:
        sent_ref[...] = closed(before)
    else:
        chip = joined(arrived, chip_ref[...])
        chip_out[...] = chip
        sent_ref[...] = closed(chip)


def join(chip, before, arrived, start, last, deps):
    block = pl.BlockSpec(chip.shape, lambda b: (0, 0, 0))
    return pl.pallas_call(
        functools.partial(join_kernel, start, last),
        grid=(1,),
        in_specs=[block] * 3 + untouched(deps),
        out_specs=[block] * 3,
        out_shape=[
            jax.ShapeDtypeStruct(chip.shape, jnp.float32),
            jax.ShapeDtypeStruct(chip.shape, jnp.float32),
            jax.ShapeDtypeStruct(chip.shape, jnp.bfloat16),
        ],
        compiler_params=params(),
        cost_estimate=cheap(),
        name="join",
    )(chip, before, arrived, *deps)


def mix_local_kernel(query_ref, key_ref, value_ref, col_ref, row_ref, first_ref, *rest):
    out_ref = rest[-1]
    rows = query_ref.shape[0]
    row = lax.broadcasted_iota(jnp.int32, (SUB, SUB), 0)
    col = lax.broadcasted_iota(jnp.int32, (SUB, SUB), 1)
    causal = col <= row
    for at in range(0, rows, SUB):
        here = slice(at, at + SUB)
        tiles_out = [None] * (WIDE // LANES)
        for head, (start, width, place) in enumerate(WINDOWS):
            lanes = slice(start, start + width)
            query = query_ref[here, lanes]
            query = jnp.where(head_lanes(query.shape, place), query, jnp.zeros_like(query))
            down = col_ref[0, here, head : head + 1]
            score = lax.dot_general(
                query,
                key_ref[here, lanes],
                (((1,), (1,)), ((), ())),
                preferred_element_type=jnp.float32,
            )
            gap = jnp.where(causal, down - row_ref[0, head : head + 1, here], -jnp.inf)
            mixing = (score * jnp.exp(gap)).astype(jnp.bfloat16)
            result = jnp.dot(mixing, value_ref[here, lanes], preferred_element_type=jnp.float32)
            if at:
                since = down - col_ref[0, at - 1 : at, head : head + 1]
                scaled = (query.astype(jnp.float32) * jnp.exp(since)).astype(jnp.bfloat16)
                result = result + jnp.dot(
                    scaled, widen(first_ref[head], width, place), preferred_element_type=jnp.float32
                )
            spread(jnp.where(head_lanes(result.shape, place), result, 0.0), start, tiles_out)
        for tile, piece in enumerate(tiles_out):
            out_ref[here, tile * LANES : (tile + 1) * LANES] = piece


def mix_local(query, key, value, decay_cols, decay_rows, first, deps):
    rows, width = query.shape
    block = pl.BlockSpec((rows, WIDE), lambda b: (0, b))
    return pl.pallas_call(
        mix_local_kernel,
        grid=(width // WIDE,),
        in_specs=[
            block,
            block,
            block,
            pl.BlockSpec((1, rows, BUNDLE), lambda b: (b, 0, 0)),
            pl.BlockSpec((1, BUNDLE, rows), lambda b: (b, 0, 0)),
            pl.BlockSpec((BUNDLE, DH, LANES), lambda b: (b, 0, 0)),
        ]
        + untouched(deps),
        out_specs=block,
        out_shape=jax.ShapeDtypeStruct((rows, width), jnp.float32),
        compiler_params=params(),
        cost_estimate=cheap(),
        name="mix_local",
    )(query, key, value, decay_cols, decay_rows, first, *deps)


def mix_final_kernel(half, info, query_ref, local_ref, col_ref, own_ref, sent_ref, other_ref, *rest):
    out_ref = rest[-1]
    rows = query_ref.shape[0]
    core = lax.rem(info[0], 2)
    mine = (pl.program_id(0) >= half).astype(jnp.int32) == core
    states = []
    for head, (_, width, place) in enumerate(WINDOWS):
        state = jnp.where(mine, own_ref[head], opened(sent_ref[head]))
        state = jnp.where(core == 0, state, joined(state, opened(other_ref[head])))
        states.append(widen(state, width, place))
    for at in range(0, rows, SUB):
        here = slice(at, at + SUB)
        tiles_out = [None] * (WIDE // LANES)
        for head, (start, width, place) in enumerate(WINDOWS):
            lanes = slice(start, start + width)
            inside = head_lanes((SUB, width), place)
            query = jnp.where(inside, query_ref[here, lanes].astype(jnp.float32), 0.0)
            scaled = (query * jnp.exp(col_ref[0, here, head : head + 1])).astype(jnp.bfloat16)
            result = jnp.dot(scaled, states[head], preferred_element_type=jnp.float32)
            result = jnp.where(inside, result + local_ref[here, lanes], 0.0)
            square = jnp.sum(result * result, axis=1, keepdims=True) * (1.0 / DH)
            factor = lax.rsqrt(square + EPS_NORM)
            spread(result * factor, start, tiles_out)
        for tile, piece in enumerate(tiles_out):
            out_ref[here, tile * LANES : (tile + 1) * LANES] = piece.astype(out_ref.dtype)


def mix_final(info, query, local, decay_cols, own, sent, other, deps):
    rows, width = query.shape
    bundles = width // WIDE
    half = bundles // 2
    block = pl.BlockSpec((rows, WIDE), lambda b, _: (0, b))
    states = pl.BlockSpec((BUNDLE, DH, LANES), lambda b, _: (b, 0, 0))
    halves = pl.BlockSpec((BUNDLE, DH, LANES), lambda b, _: (lax.rem(b, half), 0, 0))
    return pl.pallas_call(
        functools.partial(mix_final_kernel, half),
        grid_spec=pltpu.PrefetchScalarGridSpec(
            num_scalar_prefetch=1,
            grid=(bundles,),
            in_specs=[
                block,
                block,
                pl.BlockSpec((1, rows, BUNDLE), lambda b, _: (b, 0, 0)),
                halves,
                halves,
                states,
            ]
            + untouched(deps),
            out_specs=block,
        ),
        out_shape=jax.ShapeDtypeStruct((rows, width), jnp.bfloat16),
        compiler_params=params(),
        cost_estimate=cheap(),
        name="mix_final",
    )(info, query, local, decay_cols, own, sent, other, *deps)


def group_sizes(bundles):
    if bundles == 8:
        return [2, 2, 3, 1]
    return [1] * bundles


def per_device(query1, key1, value1, log_decay, out_weight, query2, key2, value2):
    rows, width = query1.shape
    bundles = width // WIDE
    count = lax.axis_size("ctx")
    position = lax.axis_index("ctx")
    info = jnp.full((1,), position, jnp.int32)

    def moved(value, pairs):
        return lax.ppermute(value, "ctx", [(s, t) for s, t in pairs if 0 <= t < count])

    everyone = range(count)
    step_pairs = [(s, s + 3 if s % 2 else s + 1) for s in everyone]
    chip_pairs = [(s, s + 2) for s in everyone if s % 4 != 3]
    back_pairs = [(s, s - 1) for s in everyone if s % 4 == 2 and s > 2]
    swap_pairs = [(s, s ^ 1) for s in everyone]

    sizes = group_sizes(bundles)
    groups = len(sizes)
    bases = [sum(sizes[:g]) for g in range(groups)]
    near, chip, back, mid, swap = {}, {}, {}, {}, {}
    done = {"last": [], "attended": None}

    def do_pack(group):
        if group < groups:
            sent = pack(key2, value2, bases[group], sizes[group], done["last"])
            near[group] = moved(sent, step_pairs)
            chip[group] = moved(sent, chip_pairs)
            done["last"] = [sent]

    def do_back(group):
        if group < groups:
            near[group] = gate(near[group], done["last"])
            done["last"] = [near[group]]
            back[group] = moved(near[group], back_pairs)

    def do_pick(group):
        if group < groups:
            mid[group] = pick(info, chip[group], back[group], done["last"])
            swap[group] = moved(mid[group], swap_pairs)
            done["last"] = [mid[group]]

    def do_attend(group):
        if group < groups:
            done["attended"] = attend(
                info, query2, key2, value2, near[group], mid[group], swap[group],
                done["attended"], bases[group], done["last"],
            )
            done["last"] = [done["attended"]]

    light = {"distance": 1, "before": None}

    def do_state():
        running = jnp.cumsum(log_decay, axis=0)
        light["cols"] = running.reshape(rows, bundles, BUNDLE).transpose(1, 0, 2)
        light["rows"] = running.T.reshape(bundles, BUNDLE, rows)
        exact, first, sent = local_state(key1, value1, light["rows"], done["last"])
        light["first"] = first
        light["other"] = moved(sent, swap_pairs)
        light["exact"] = exact
        done["last"] = [sent]

    def do_chip():
        light["chip"], sent = chip_state(info, light["exact"], light["other"], done["last"])
        light["arrived"] = moved(sent, [(s, s + 2) for s in everyone])
        light["distance"] = 1
        done["last"] = [sent]

    def do_join():
        if light["distance"] < count // 2:
            start = light["distance"] == 1
            light["distance"] *= 2
            last = light["distance"] >= count // 2
            before = light["chip"] if start else light["before"]
            light["chip"], light["before"], sent = join(
                light["chip"], before, light["arrived"], start, last, done["last"]
            )
            pairs = swap_pairs if last else [(s, s + 2 * light["distance"]) for s in everyone]
            light["arrived"] = moved(sent, pairs)
            done["last"] = [sent]

    def do_mix_local():
        light["local"] = mix_local(
            query1, key1, value1, light["cols"], light["rows"], light["first"], done["last"]
        )
        done["last"] = [light["local"]]

    def do_mix_final():
        while light["distance"] < count // 2:
            do_join()
        light["normed"] = mix_final(
            info, query1, light["local"], light["cols"], light["before"], light["arrived"],
            light["other"], done["last"],
        )
        done["last"] = [light["normed"]]

    def do_project():
        product = jnp.dot(light["normed"], out_weight, preferred_element_type=jnp.float32)
        product = product.astype(jnp.bfloat16)
        done["linear"] = lax.psum_scatter(product, "head", scatter_dimension=0, tiled=True)
        done["last"] = [product]

    def wait_chip(group):
        done["last"] = done["last"] + [chip[group]]

    do_pack(0)
    do_pack(1)
    do_state()
    do_back(0)
    do_mix_local()
    wait_chip(0)
    do_chip()
    do_back(1)
    do_pick(0)
    do_join()
    do_attend(0)
    do_join()
    do_join()
    do_pack(2)
    do_pick(1)
    do_mix_final()
    do_project()
    do_back(2)
    do_pack(3)
    do_attend(1)
    do_back(3)
    do_pick(2)
    do_attend(2)
    do_pick(3)
    do_attend(3)
    return (done["linear"], done["attended"])


def solution(mesh):
    in_specs = (
        P("ctx", "head"),
        P("ctx", "head"),
        P("ctx", "head"),
        P("ctx", "head"),
        P("head", None),
        P("ctx", "head"),
        P("ctx", "head"),
        P("ctx", "head"),
    )
    out_specs = (P(("ctx", "head"), None), P("ctx", "head"))
    return jax.shard_map(
        per_device, mesh=mesh, in_specs=in_specs, out_specs=out_specs, check_vma=False
    )
```

```python
import functools
import math

import jax
import jax.numpy as jnp
from jax import lax
from jax.experimental import pallas as pl
from jax.experimental.pallas import tpu as pltpu
from jax.sharding import PartitionSpec as P

DH = 96
SUB = 256
BUNDLE = 4
WIDE = BUNDLE * DH
LANES = 128
EPS_NORM = 1e-06
VMEM_BYTES = 63 * 1024 * 1024
WINDOWS = ((0, 128, 0), (0, 256, 96), (128, 256, 64), (256, 128, 32))


def cheap():
    return pl.CostEstimate(flops=1000, bytes_accessed=1000, transcendentals=0)


def params():
    return pltpu.CompilerParams(vmem_limit_bytes=VMEM_BYTES)


def untouched(deps):
    return [pl.BlockSpec(memory_space=pl.ANY)] * len(deps)


def gate_kernel(*refs):
    del refs


def gate(value, deps):
    return pl.pallas_call(
        gate_kernel,
        in_specs=untouched([value, *deps]),
        out_specs=pl.BlockSpec(memory_space=pl.ANY),
        out_shape=jax.ShapeDtypeStruct(value.shape, value.dtype),
        input_output_aliases={0: 0},
        compiler_params=params(),
        cost_estimate=cheap(),
        name="gate",
    )(value, *deps)


def head_lanes(shape, start):
    lane = lax.broadcasted_iota(jnp.int32, shape, len(shape) - 1)
    return (lane >= start) & (lane < start + DH)


def pack_kernel(key_ref, value_ref, *rest):
    out_ref = rest[-1]
    out_ref[0] = key_ref[...]
    out_ref[1] = value_ref[...]


def pack(key, value, base, bundles, deps):
    rows = key.shape[0]
    block = pl.BlockSpec((rows, WIDE), lambda b: (0, base + b))
    return pl.pallas_call(
        pack_kernel,
        grid=(bundles,),
        in_specs=[block, block] + untouched(deps),
        out_specs=pl.BlockSpec((2, rows, WIDE), lambda b: (0, 0, b)),
        out_shape=jax.ShapeDtypeStruct((2, rows, bundles * WIDE), key.dtype),
        compiler_params=params(),
        cost_estimate=cheap(),
        name="pack",
    )(key, value, *deps)


def pick_kernel(info, chip_ref, back_ref, *rest):
    out_ref = rest[-1]
    from_back = lax.rem(info[0], 4) == 1

    @pl.when(from_back)
    def _():
        out_ref[...] = back_ref[...]

    @pl.when(jnp.logical_not(from_back))
    def _():
        out_ref[...] = chip_ref[...]


def pick(info, chip, back, deps):
    _, rows, width = chip.shape
    shape = (1, rows, WIDE)

    def from_chip(i, b, info):
        other = lax.rem(info[0], 4) == 1
        return (jnp.where(other, 0, i), 0, jnp.where(other, 0, b))

    def from_back(i, b, info):
        other = lax.rem(info[0], 4) != 1
        return (jnp.where(other, 0, i), 0, jnp.where(other, 0, b))

    return pl.pallas_call(
        pick_kernel,
        grid_spec=pltpu.PrefetchScalarGridSpec(
            num_scalar_prefetch=1,
            grid=(2, width // WIDE),
            in_specs=[pl.BlockSpec(shape, from_chip), pl.BlockSpec(shape, from_back)]
            + untouched(deps),
            out_specs=pl.BlockSpec(shape, lambda i, b, _: (i, 0, b)),
        ),
        out_shape=jax.ShapeDtypeStruct(chip.shape, chip.dtype),
        compiler_params=params(),
        cost_estimate=cheap(),
        name="pick",
    )(info, chip, back, *deps)


def attend_body(exists, query_ref, slots, out_ref):
    rows = query_ref.shape[0]
    scale = math.log2(math.e) / math.sqrt(DH)
    key_at = lax.broadcasted_iota(jnp.int32, (SUB, SUB), 0)
    query_at = lax.broadcasted_iota(jnp.int32, (SUB, SUB), 1)
    newer, older = key_at > query_at, key_at <= query_at
    low = jnp.float32(-1e30)
    values = [value_ref[...].T for _, value_ref in slots]
    ones = jnp.ones((16, rows), values[0].dtype)
    units = [(part, head) for part in range(rows // SUB) for head in range(BUNDLE)]

    def spans(part):
        first = part * SUB
        return [(first, rows), (0, rows), (0, rows), (0, first + SUB)]

    def score_unit(part, head):
        start, width, place = WINDOWS[head]
        lanes = slice(start, start + width)
        query = query_ref[part * SUB : (part + 1) * SUB, lanes]
        query = jnp.where(head_lanes(query.shape, place), query, jnp.zeros_like(query))
        tiles, peak = [], None
        for slot in range(4):
            begin, end = spans(part)[slot]
            tiles.append([])
            top = None
            for at in range(begin, end, SUB):
                score = lax.dot_general(
                    slots[slot][0][at : at + SUB, lanes],
                    query,
                    (((1,), (1,)), ((), ())),
                    preferred_element_type=jnp.float32,
                )
                if slot == 0 and at == begin:
                    score = jnp.where(newer, score, low)
                if slot == 3 and at == end - SUB:
                    score = jnp.where(older, score, low)
                tiles[slot].append(score)
                piece = jnp.max(score, axis=0, keepdims=True)
                top = piece if top is None else jnp.maximum(top, piece)
            if slot < 3:
                top = jnp.where(exists[slot], top, low)
            peak = top if peak is None else jnp.maximum(peak, top)
        return tiles, peak * scale

    def value_unit(part, head, tiles, peak):
        result = None
        for slot in range(4):
            begin, end = spans(part)[slot]
            shift = peak
            if slot < 3:
                shift = jnp.where(exists[slot], peak, jnp.float32(1e30))
            weights = [jnp.exp2(tile * scale - shift).astype(jnp.bfloat16) for tile in tiles[slot]]
            weight = weights[0] if len(weights) == 1 else jnp.concatenate(weights, axis=0)
            value = values[slot][head * DH : (head + 1) * DH, begin:end]
            value = jnp.concatenate([value, ones[:, begin:end]], axis=0)
            term = jnp.dot(value, weight, preferred_element_type=jnp.float32)
            result = term if result is None else result + term
        return result[:DH] * (1.0 / result[DH : DH + 1])

    ready = score_unit(*units[0])
    heads = []
    for index, (part, head) in enumerate(units):
        following = score_unit(*units[index + 1]) if index + 1 < len(units) else None
        heads.append(value_unit(part, head, *ready))
        if head == BUNDLE - 1:
            result = jnp.concatenate(heads, axis=0).T
            out_ref[part * SUB : (part + 1) * SUB, :] = result.astype(out_ref.dtype)
            heads = []
        ready = following


def attend_kernel(info, query_ref, key_ref, value_ref, near_ref, mid_ref, swap_ref, *rest):
    out_ref = rest[-1]
    position = info[0]
    exists = [position >= 3, position >= 2, position >= 1]
    own = (key_ref, value_ref)
    near, mid, swap = [(r.at[0], r.at[1]) for r in (near_ref, mid_ref, swap_ref)]
    core = lax.rem(position, 2)

    @pl.when(core == 0)
    def _():
        attend_body(exists, query_ref, [near, mid, swap, own], out_ref)

    @pl.when(core == 1)
    def _():
        attend_body(exists, query_ref, [swap, mid, near, own], out_ref)


def attend(info, query, key, value, near, mid, swap, out, base, deps):
    rows = query.shape[0]
    block = pl.BlockSpec((rows, WIDE), lambda b, _: (0, base + b))
    pair = pl.BlockSpec((2, rows, WIDE), lambda b, _: (0, 0, b))
    filled = [] if out is None else [out]
    return pl.pallas_call(
        attend_kernel,
        grid_spec=pltpu.PrefetchScalarGridSpec(
            num_scalar_prefetch=1,
            grid=(near.shape[2] // WIDE,),
            in_specs=[block, block, block, pair, pair, pair] + untouched([*filled, *deps]),
            out_specs=block,
        ),
        out_shape=jax.ShapeDtypeStruct(query.shape, query.dtype),
        input_output_aliases={7: 0} if filled else {},
        compiler_params=params(),
        cost_estimate=cheap(),
        name="attend",
    )(info, query, key, value, near, mid, swap, *filled, *deps)


def opened(message):
    wide = message.astype(jnp.float32)
    lane = lax.broadcasted_iota(jnp.int32, wide.shape, wide.ndim - 1)
    return jnp.where(lane == DH, wide + wide[..., DH + 1 : DH + 2], wide)


def closed(exact):
    lane = lax.broadcasted_iota(jnp.int32, exact.shape, exact.ndim - 1)
    decay = exact[..., DH : DH + 1]
    rest = decay - decay.astype(jnp.bfloat16).astype(jnp.float32)
    return jnp.where(lane == DH + 1, rest, exact).astype(jnp.bfloat16)


def joined(earlier, later):
    lane = lax.broadcasted_iota(jnp.int32, earlier.shape, earlier.ndim - 1)
    kept = jnp.exp(later[..., DH : DH + 1])
    return jnp.where(lane == DH, earlier + later, earlier * kept + later)


def state_kernel(key_ref, value_ref, decay_ref, *rest):
    exact_ref, first_ref, sent_ref = rest[-3:]
    rows = key_ref.shape[0]
    lane = lax.broadcasted_iota(jnp.int32, (DH, LANES), 1)
    value_t = value_ref[...].T
    for head, (start, width, place) in enumerate(WINDOWS):
        lanes = slice(start, start + width)
        state, before = None, None
        for at in range(0, rows, SUB):
            running = decay_ref[0, head : head + 1, at : at + SUB]
            anchor = running[:, SUB - 1 :]
            value = value_t[head * DH : (head + 1) * DH, at : at + SUB].astype(jnp.float32)
            update = jnp.dot(
                (value * jnp.exp(anchor - running)).astype(jnp.bfloat16),
                key_ref[at : at + SUB, lanes],
                preferred_element_type=jnp.float32,
            )
            if at + SUB == rows:
                first_ref[head] = narrow(state, place)
            state = update if state is None else state * jnp.exp(anchor - before) + update
            before = anchor
        exact = jnp.where(lane == DH, before, narrow(state, place))
        exact_ref[head] = exact
        sent_ref[head] = closed(exact)


def narrow(state, place):
    width = state.shape[1]
    if place:
        state = pltpu.roll(state, width - place, axis=1)
    state = state[:, :LANES]
    lane = lax.broadcasted_iota(jnp.int32, state.shape, 1)
    return jnp.where(lane < DH, state, 0.0)


def local_state(key, value, decay_rows, deps):
    rows, width = key.shape
    bundles = width // WIDE
    block = pl.BlockSpec((rows, WIDE), lambda b: (0, b))
    out = pl.BlockSpec((BUNDLE, DH, LANES), lambda b: (b, 0, 0))
    shape = (bundles * BUNDLE, DH, LANES)
    return pl.pallas_call(
        state_kernel,
        grid=(bundles,),
        in_specs=[block, block, pl.BlockSpec((1, BUNDLE, rows), lambda b: (b, 0, 0))]
        + untouched(deps),
        out_specs=[out, out, out],
        out_shape=[
            jax.ShapeDtypeStruct(shape, jnp.float32),
            jax.ShapeDtypeStruct(shape, jnp.float32),
            jax.ShapeDtypeStruct(shape, jnp.bfloat16),
        ],
        compiler_params=params(),
        cost_estimate=cheap(),
        name="local_state",
    )(key, value, decay_rows, *deps)


def chip_state_kernel(info, exact_ref, other_ref, *rest):
    chip_ref, sent_ref = rest[-2:]
    even = lax.rem(info[0], 2) == 0
    mine, other = exact_ref[...], opened(other_ref[...])
    chip = joined(jnp.where(even, mine, other), jnp.where(even, other, mine))
    chip_ref[...] = chip
    sent_ref[...] = closed(chip)


def chip_state(info, exact, other, deps):
    half = exact.shape[0] // 2
    shape = (half, DH, LANES)
    block = pl.BlockSpec(shape, lambda b, _: (0, 0, 0))

    def mine(b, info):
        return (lax.rem(info[0], 2), 0, 0)

    return pl.pallas_call(
        chip_state_kernel,
        grid_spec=pltpu.PrefetchScalarGridSpec(
            num_scalar_prefetch=1,
            grid=(1,),
            in_specs=[pl.BlockSpec(shape, mine)] * 2 + untouched(deps),
            out_specs=[block, block],
        ),
        out_shape=[
            jax.ShapeDtypeStruct(shape, jnp.float32),
            jax.ShapeDtypeStruct(shape, jnp.bfloat16),
        ],
        compiler_params=params(),
        cost_estimate=cheap(),
        name="chip_state",
    )(info, exact, other, *deps)


def join_kernel(start, last, chip_ref, before_ref, arrived_ref, *rest):
    chip_out, before_out, sent_ref = rest[-3:]
    arrived = opened(arrived_ref[...])
    before = arrived if start else joined(arrived, before_ref[...])
    before_out[...] = before
    if last:
        sent_ref[...] = closed(before)
    else:
        chip = joined(arrived, chip_ref[...])
        chip_out[...] = chip
        sent_ref[...] = closed(chip)


def join(chip, before, arrived, start, last, deps):
    block = pl.BlockSpec(chip.shape, lambda b: (0, 0, 0))
    return pl.pallas_call(
        functools.partial(join_kernel, start, last),
        grid=(1,),
        in_specs=[block] * 3 + untouched(deps),
        out_specs=[block] * 3,
        out_shape=[
            jax.ShapeDtypeStruct(chip.shape, jnp.float32),
            jax.ShapeDtypeStruct(chip.shape, jnp.float32),
            jax.ShapeDtypeStruct(chip.shape, jnp.bfloat16),
        ],
        compiler_params=params(),
        cost_estimate=cheap(),
        name="join",
    )(chip, before, arrived, *deps)


def mix_local_kernel(query_ref, key_ref, value_ref, col_ref, row_ref, first_ref, *rest):
    out_ref = rest[-1]
    rows = query_ref.shape[0]
    key_at = lax.broadcasted_iota(jnp.int32, (SUB, SUB), 0)
    query_at = lax.broadcasted_iota(jnp.int32, (SUB, SUB), 1)
    causal = key_at <= query_at
    value_t, query_t = value_ref[...].T, query_ref[...].T
    for at in range(0, rows, SUB):
        here = slice(at, at + SUB)
        for head, (start, width, place) in enumerate(WINDOWS):
            lanes = slice(start, start + width)
            features = slice(head * DH, (head + 1) * DH)
            query = query_ref[here, lanes]
            query = jnp.where(head_lanes(query.shape, place), query, jnp.zeros_like(query))
            score = lax.dot_general(
                key_ref[here, lanes],
                query,
                (((1,), (1,)), ((), ())),
                preferred_element_type=jnp.float32,
            )
            along = row_ref[0, head : head + 1, here]
            gap = jnp.where(causal, along - col_ref[0, here, head : head + 1], -jnp.inf)
            mixing = (score * jnp.exp(gap)).astype(jnp.bfloat16)
            result = jnp.dot(value_t[features, here], mixing, preferred_element_type=jnp.float32)
            if at:
                since = along - row_ref[0, head : head + 1, at - 1 : at]
                scaled = query_t[features, here].astype(jnp.float32) * jnp.exp(since)
                result = result + jnp.dot(
                    first_ref[head][:, :DH].astype(jnp.bfloat16),
                    scaled.astype(jnp.bfloat16),
                    preferred_element_type=jnp.float32,
                )
            out_ref[features, here] = result


def mix_local(query, key, value, decay_cols, decay_rows, first, deps):
    rows, width = query.shape
    block = pl.BlockSpec((rows, WIDE), lambda b: (0, b))
    return pl.pallas_call(
        mix_local_kernel,
        grid=(width // WIDE,),
        in_specs=[
            block,
            block,
            block,
            pl.BlockSpec((1, rows, BUNDLE), lambda b: (b, 0, 0)),
            pl.BlockSpec((1, BUNDLE, rows), lambda b: (b, 0, 0)),
            pl.BlockSpec((BUNDLE, DH, LANES), lambda b: (b, 0, 0)),
        ]
        + untouched(deps),
        out_specs=pl.BlockSpec((WIDE, rows), lambda b: (b, 0)),
        out_shape=jax.ShapeDtypeStruct((width, rows), jnp.float32),
        compiler_params=params(),
        cost_estimate=cheap(),
        name="mix_local",
    )(query, key, value, decay_cols, decay_rows, first, *deps)


def mix_final_kernel(half, info, query_ref, local_ref, row_ref, own_ref, sent_ref, other_ref, *rest):
    out_ref = rest[-1]
    core = lax.rem(info[0], 2)
    mine = (pl.program_id(0) >= half).astype(jnp.int32) == core
    query_t = query_ref[...].T
    heads = []
    for head in range(BUNDLE):
        features = slice(head * DH, (head + 1) * DH)
        state = jnp.where(mine, own_ref[head], opened(sent_ref[head]))
        state = jnp.where(core == 0, state, joined(state, opened(other_ref[head])))
        scaled = query_t[features, :].astype(jnp.float32) * jnp.exp(row_ref[0, head : head + 1, :])
        result = local_ref[features, :] + jnp.dot(
            state[:, :DH].astype(jnp.bfloat16),
            scaled.astype(jnp.bfloat16),
            preferred_element_type=jnp.float32,
        )
        square = jnp.sum(result * result, axis=0, keepdims=True) * (1.0 / DH)
        heads.append(result * lax.rsqrt(square + EPS_NORM))
    out_ref[...] = jnp.concatenate(heads, axis=0).T.astype(out_ref.dtype)


def mix_final(info, query, local, decay_rows, own, sent, other, deps):
    rows, width = query.shape
    bundles = width // WIDE
    half = bundles // 2
    block = pl.BlockSpec((rows, WIDE), lambda b, _: (0, b))
    states = pl.BlockSpec((BUNDLE, DH, LANES), lambda b, _: (b, 0, 0))
    halves = pl.BlockSpec((BUNDLE, DH, LANES), lambda b, _: (lax.rem(b, half), 0, 0))
    return pl.pallas_call(
        functools.partial(mix_final_kernel, half),
        grid_spec=pltpu.PrefetchScalarGridSpec(
            num_scalar_prefetch=1,
            grid=(bundles,),
            in_specs=[
                block,
                pl.BlockSpec((WIDE, rows), lambda b, _: (b, 0)),
                pl.BlockSpec((1, BUNDLE, rows), lambda b, _: (b, 0, 0)),
                halves,
                halves,
                states,
            ]
            + untouched(deps),
            out_specs=block,
        ),
        out_shape=jax.ShapeDtypeStruct((rows, width), jnp.bfloat16),
        compiler_params=params(),
        cost_estimate=cheap(),
        name="mix_final",
    )(info, query, local, decay_rows, own, sent, other, *deps)


def group_sizes(bundles):
    if bundles == 8:
        return [2, 2, 3, 1]
    return [1] * bundles


def per_device(query1, key1, value1, log_decay, out_weight, query2, key2, value2):
    rows, width = query1.shape
    bundles = width // WIDE
    count = lax.axis_size("ctx")
    position = lax.axis_index("ctx")
    info = jnp.full((1,), position, jnp.int32)

    def moved(value, pairs):
        return lax.ppermute(value, "ctx", [(s, t) for s, t in pairs if 0 <= t < count])

    everyone = range(count)
    step_pairs = [(s, s + 3 if s % 2 else s + 1) for s in everyone]
    chip_pairs = [(s, s + 2) for s in everyone if s % 4 != 3]
    back_pairs = [(s, s - 1) for s in everyone if s % 4 == 2 and s > 2]
    swap_pairs = [(s, s ^ 1) for s in everyone]

    sizes = group_sizes(bundles)
    groups = len(sizes)
    bases = [sum(sizes[:g]) for g in range(groups)]
    near, chip, back, mid, swap = {}, {}, {}, {}, {}
    done = {"last": [], "attended": None}

    def do_pack(group):
        if group < groups:
            sent = pack(key2, value2, bases[group], sizes[group], done["last"])
            near[group] = moved(sent, step_pairs)
            chip[group] = moved(sent, chip_pairs)
            done["last"] = [sent]

    def do_back(group):
        if group < groups:
            near[group] = gate(near[group], done["last"])
            done["last"] = [near[group]]
            back[group] = moved(near[group], back_pairs)

    def do_pick(group):
        if group < groups:
            mid[group] = pick(info, chip[group], back[group], done["last"])
            swap[group] = moved(mid[group], swap_pairs)
            done["last"] = [mid[group]]

    def do_attend(group):
        if group < groups:
            done["attended"] = attend(
                info, query2, key2, value2, near[group], mid[group], swap[group],
                done["attended"], bases[group], done["last"],
            )
            done["last"] = [done["attended"]]

    light = {"distance": 1, "before": None}

    def do_state():
        running = jnp.cumsum(log_decay, axis=0)
        light["cols"] = running.reshape(rows, bundles, BUNDLE).transpose(1, 0, 2)
        light["rows"] = running.T.reshape(bundles, BUNDLE, rows)
        exact, first, sent = local_state(key1, value1, light["rows"], done["last"])
        light["first"] = first
        light["other"] = moved(sent, swap_pairs)
        light["exact"] = exact
        done["last"] = [sent]

    def do_chip():
        light["chip"], sent = chip_state(info, light["exact"], light["other"], done["last"])
        light["arrived"] = moved(sent, [(s, s + 2) for s in everyone])
        light["distance"] = 1
        done["last"] = [sent]

    def do_join():
        if light["distance"] < count // 2:
            start = light["distance"] == 1
            light["distance"] *= 2
            last = light["distance"] >= count // 2
            before = light["chip"] if start else light["before"]
            light["chip"], light["before"], sent = join(
                light["chip"], before, light["arrived"], start, last, done["last"]
            )
            pairs = swap_pairs if last else [(s, s + 2 * light["distance"]) for s in everyone]
            light["arrived"] = moved(sent, pairs)
            done["last"] = [sent]

    def do_mix_local():
        light["local"] = mix_local(
            query1, key1, value1, light["cols"], light["rows"], light["first"], done["last"]
        )
        done["last"] = [light["local"]]

    def do_mix_final():
        while light["distance"] < count // 2:
            do_join()
        light["normed"] = mix_final(
            info, query1, light["local"], light["rows"], light["before"], light["arrived"],
            light["other"], done["last"],
        )
        done["last"] = [light["normed"]]

    def do_project():
        product = jnp.dot(light["normed"], out_weight, preferred_element_type=jnp.float32)
        product = product.astype(jnp.bfloat16)
        done["linear"] = lax.psum_scatter(product, "head", scatter_dimension=0, tiled=True)
        done["last"] = [product]

    def wait_chip(group):
        done["last"] = done["last"] + [chip[group]]

    do_pack(0)
    do_pack(1)
    do_state()
    do_back(0)
    do_mix_local()
    wait_chip(0)
    do_chip()
    do_back(1)
    do_pick(0)
    do_join()
    do_attend(0)
    do_join()
    do_join()
    do_pack(2)
    do_pick(1)
    do_mix_final()
    do_project()
    do_back(2)
    do_pack(3)
    do_attend(1)
    do_back(3)
    do_pick(2)
    do_attend(2)
    do_pick(3)
    do_attend(3)
    return (done["linear"], done["attended"])


def solution(mesh):
    in_specs = (
        P("ctx", "head"),
        P("ctx", "head"),
        P("ctx", "head"),
        P("ctx", "head"),
        P("head", None),
        P("ctx", "head"),
        P("ctx", "head"),
        P("ctx", "head"),
    )
    out_specs = (P(("ctx", "head"), None), P("ctx", "head"))
    return jax.shard_map(
        per_device, mesh=mesh, in_specs=in_specs, out_specs=out_specs, check_vma=False
    )
```

```python
import functools
import math

import jax
import jax.numpy as jnp
from jax import lax
from jax.experimental import pallas as pl
from jax.experimental.pallas import tpu as pltpu
from jax.sharding import PartitionSpec as P

DH = 96
SUB = 256
BUNDLE = 4
WIDE = BUNDLE * DH
LANES = 128
EPS_NORM = 1e-06
VMEM_BYTES = 63 * 1024 * 1024
WINDOWS = ((0, 128, 0), (0, 256, 96), (128, 256, 64), (256, 128, 32))


def cheap():
    return pl.CostEstimate(flops=1000, bytes_accessed=1000, transcendentals=0)


def params():
    return pltpu.CompilerParams(vmem_limit_bytes=VMEM_BYTES)


def untouched(deps):
    return [pl.BlockSpec(memory_space=pl.ANY)] * len(deps)


def gate_kernel(*refs):
    del refs


def gate(value, deps):
    return pl.pallas_call(
        gate_kernel,
        in_specs=untouched([value, *deps]),
        out_specs=pl.BlockSpec(memory_space=pl.ANY),
        out_shape=jax.ShapeDtypeStruct(value.shape, value.dtype),
        input_output_aliases={0: 0},
        compiler_params=params(),
        cost_estimate=cheap(),
        name="gate",
    )(value, *deps)


def head_lanes(shape, start):
    lane = lax.broadcasted_iota(jnp.int32, shape, len(shape) - 1)
    return (lane >= start) & (lane < start + DH)


def pack_kernel(key_ref, value_ref, *rest):
    out_ref = rest[-1]
    out_ref[0] = key_ref[...]
    out_ref[1] = value_ref[...]


def pack(key, value, base, bundles, deps):
    rows = key.shape[0]
    block = pl.BlockSpec((rows, WIDE), lambda b: (0, base + b))
    return pl.pallas_call(
        pack_kernel,
        grid=(bundles,),
        in_specs=[block, block] + untouched(deps),
        out_specs=pl.BlockSpec((2, rows, WIDE), lambda b: (0, 0, b)),
        out_shape=jax.ShapeDtypeStruct((2, rows, bundles * WIDE), key.dtype),
        compiler_params=params(),
        cost_estimate=cheap(),
        name="pack",
    )(key, value, *deps)


def pick_kernel(info, chip_ref, back_ref, *rest):
    out_ref = rest[-1]
    from_back = lax.rem(info[0], 4) == 1

    @pl.when(from_back)
    def _():
        out_ref[...] = back_ref[...]

    @pl.when(jnp.logical_not(from_back))
    def _():
        out_ref[...] = chip_ref[...]


def pick(info, chip, back, deps):
    _, rows, width = chip.shape
    shape = (1, rows, WIDE)

    def from_chip(i, b, info):
        other = lax.rem(info[0], 4) == 1
        return (jnp.where(other, 0, i), 0, jnp.where(other, 0, b))

    def from_back(i, b, info):
        other = lax.rem(info[0], 4) != 1
        return (jnp.where(other, 0, i), 0, jnp.where(other, 0, b))

    return pl.pallas_call(
        pick_kernel,
        grid_spec=pltpu.PrefetchScalarGridSpec(
            num_scalar_prefetch=1,
            grid=(2, width // WIDE),
            in_specs=[pl.BlockSpec(shape, from_chip), pl.BlockSpec(shape, from_back)]
            + untouched(deps),
            out_specs=pl.BlockSpec(shape, lambda i, b, _: (i, 0, b)),
        ),
        out_shape=jax.ShapeDtypeStruct(chip.shape, chip.dtype),
        compiler_params=params(),
        cost_estimate=cheap(),
        name="pick",
    )(info, chip, back, *deps)


def attend_body(exists, query_ref, slots, out_ref):
    rows = query_ref.shape[0]
    scale = math.log2(math.e) / math.sqrt(DH)
    key_at = lax.broadcasted_iota(jnp.int32, (SUB, SUB), 0)
    query_at = lax.broadcasted_iota(jnp.int32, (SUB, SUB), 1)
    newer, older = key_at > query_at, key_at <= query_at
    low = jnp.float32(-1e30)
    values = [value_ref[...].T for _, value_ref in slots]
    ones = jnp.ones((16, rows), values[0].dtype)
    units = [(part, head) for part in range(rows // SUB) for head in range(BUNDLE)]

    def spans(part):
        first = part * SUB
        return [(first, rows), (0, rows), (0, rows), (0, first + SUB)]

    def score_unit(part, head):
        start, width, place = WINDOWS[head]
        lanes = slice(start, start + width)
        query = query_ref[part * SUB : (part + 1) * SUB, lanes]
        query = jnp.where(head_lanes(query.shape, place), query, jnp.zeros_like(query))
        tiles, peak = [], None
        for slot in range(4):
            begin, end = spans(part)[slot]
            tiles.append([])
            top = None
            for at in range(begin, end, SUB):
                score = lax.dot_general(
                    slots[slot][0][at : at + SUB, lanes],
                    query,
                    (((1,), (1,)), ((), ())),
                    preferred_element_type=jnp.float32,
                )
                if slot == 0 and at == begin:
                    score = jnp.where(newer, score, low)
                if slot == 3 and at == end - SUB:
                    score = jnp.where(older, score, low)
                tiles[slot].append(score)
                piece = jnp.max(score, axis=0, keepdims=True)
                top = piece if top is None else jnp.maximum(top, piece)
            if slot < 3:
                top = jnp.where(exists[slot], top, low)
            peak = top if peak is None else jnp.maximum(peak, top)
        return tiles, peak * scale

    def value_unit(part, head, tiles, peak):
        result = None
        for slot in range(4):
            begin, end = spans(part)[slot]
            shift = peak
            if slot < 3:
                shift = jnp.where(exists[slot], peak, jnp.float32(1e30))
            weights = [jnp.exp2(tile * scale - shift).astype(jnp.bfloat16) for tile in tiles[slot]]
            weight = weights[0] if len(weights) == 1 else jnp.concatenate(weights, axis=0)
            value = values[slot][head * DH : (head + 1) * DH, begin:end]
            value = jnp.concatenate([value, ones[:, begin:end]], axis=0)
            term = jnp.dot(value, weight, preferred_element_type=jnp.float32)
            result = term if result is None else result + term
        return result[:DH] * (1.0 / result[DH : DH + 1])

    ready = score_unit(*units[0])
    heads = []
    for index, (part, head) in enumerate(units):
        following = score_unit(*units[index + 1]) if index + 1 < len(units) else None
        heads.append(value_unit(part, head, *ready))
        if head == BUNDLE - 1:
            result = jnp.concatenate(heads, axis=0).T
            out_ref[part * SUB : (part + 1) * SUB, :] = result.astype(out_ref.dtype)
            heads = []
        ready = following


def attend_kernel(info, query_ref, key_ref, value_ref, near_ref, mid_ref, swap_ref, *rest):
    out_ref = rest[-1]
    position = info[0]
    exists = [position >= 3, position >= 2, position >= 1]
    own = (key_ref, value_ref)
    near, mid, swap = [(r.at[0], r.at[1]) for r in (near_ref, mid_ref, swap_ref)]
    core = lax.rem(position, 2)

    @pl.when(core == 0)
    def _():
        attend_body(exists, query_ref, [near, mid, swap, own], out_ref)

    @pl.when(core == 1)
    def _():
        attend_body(exists, query_ref, [swap, mid, near, own], out_ref)


def attend(info, query, key, value, near, mid, swap, out, base, deps):
    rows = query.shape[0]
    block = pl.BlockSpec((rows, WIDE), lambda b, _: (0, base + b))
    pair = pl.BlockSpec((2, rows, WIDE), lambda b, _: (0, 0, b))
    filled = [] if out is None else [out]
    return pl.pallas_call(
        attend_kernel,
        grid_spec=pltpu.PrefetchScalarGridSpec(
            num_scalar_prefetch=1,
            grid=(near.shape[2] // WIDE,),
            in_specs=[block, block, block, pair, pair, pair] + untouched([*filled, *deps]),
            out_specs=block,
        ),
        out_shape=jax.ShapeDtypeStruct(query.shape, query.dtype),
        input_output_aliases={7: 0} if filled else {},
        compiler_params=params(),
        cost_estimate=cheap(),
        name="attend",
    )(info, query, key, value, near, mid, swap, *filled, *deps)


def opened(message):
    wide = message.astype(jnp.float32)
    lane = lax.broadcasted_iota(jnp.int32, wide.shape, wide.ndim - 1)
    return jnp.where(lane == DH, wide + wide[..., DH + 1 : DH + 2], wide)


def closed(exact):
    lane = lax.broadcasted_iota(jnp.int32, exact.shape, exact.ndim - 1)
    decay = exact[..., DH : DH + 1]
    rest = decay - decay.astype(jnp.bfloat16).astype(jnp.float32)
    return jnp.where(lane == DH + 1, rest, exact).astype(jnp.bfloat16)


def joined(earlier, later):
    lane = lax.broadcasted_iota(jnp.int32, earlier.shape, earlier.ndim - 1)
    kept = jnp.exp(later[..., DH : DH + 1])
    return jnp.where(lane == DH, earlier + later, earlier * kept + later)


def state_kernel(key_ref, value_ref, decay_ref, *rest):
    exact_ref, first_ref, sent_ref = rest[-3:]
    rows = key_ref.shape[0]
    lane = lax.broadcasted_iota(jnp.int32, (DH, LANES), 1)
    value_t = value_ref[...].T
    for head, (start, width, place) in enumerate(WINDOWS):
        lanes = slice(start, start + width)
        state, before = None, None
        for at in range(0, rows, SUB):
            running = decay_ref[0, head : head + 1, at : at + SUB]
            anchor = running[:, SUB - 1 :]
            value = value_t[head * DH : (head + 1) * DH, at : at + SUB].astype(jnp.float32)
            update = jnp.dot(
                (value * jnp.exp(anchor - running)).astype(jnp.bfloat16),
                key_ref[at : at + SUB, lanes],
                preferred_element_type=jnp.float32,
            )
            if at + SUB == rows:
                first_ref[head] = narrow(state, place)
            state = update if state is None else state * jnp.exp(anchor - before) + update
            before = anchor
        exact = jnp.where(lane == DH, before, narrow(state, place))
        exact_ref[head] = exact
        sent_ref[head] = closed(exact)


def narrow(state, place):
    width = state.shape[1]
    if place:
        state = pltpu.roll(state, width - place, axis=1)
    state = state[:, :LANES]
    lane = lax.broadcasted_iota(jnp.int32, state.shape, 1)
    return jnp.where(lane < DH, state, 0.0)


def local_state(key, value, decay_rows, deps):
    rows, width = key.shape
    bundles = width // WIDE
    block = pl.BlockSpec((rows, WIDE), lambda b: (0, b))
    out = pl.BlockSpec((BUNDLE, DH, LANES), lambda b: (b, 0, 0))
    shape = (bundles * BUNDLE, DH, LANES)
    return pl.pallas_call(
        state_kernel,
        grid=(bundles,),
        in_specs=[block, block, pl.BlockSpec((1, BUNDLE, rows), lambda b: (b, 0, 0))]
        + untouched(deps),
        out_specs=[out, out, out],
        out_shape=[
            jax.ShapeDtypeStruct(shape, jnp.float32),
            jax.ShapeDtypeStruct(shape, jnp.float32),
            jax.ShapeDtypeStruct(shape, jnp.bfloat16),
        ],
        compiler_params=params(),
        cost_estimate=cheap(),
        name="local_state",
    )(key, value, decay_rows, *deps)


def chip_state_kernel(info, exact_ref, other_ref, *rest):
    chip_ref, sent_ref = rest[-2:]
    even = lax.rem(info[0], 2) == 0
    mine, other = exact_ref[...], opened(other_ref[...])
    chip = joined(jnp.where(even, mine, other), jnp.where(even, other, mine))
    chip_ref[...] = chip
    sent_ref[...] = closed(chip)


def chip_state(info, exact, other, deps):
    half = exact.shape[0] // 2
    shape = (half, DH, LANES)
    block = pl.BlockSpec(shape, lambda b, _: (0, 0, 0))

    def mine(b, info):
        return (lax.rem(info[0], 2), 0, 0)

    return pl.pallas_call(
        chip_state_kernel,
        grid_spec=pltpu.PrefetchScalarGridSpec(
            num_scalar_prefetch=1,
            grid=(1,),
            in_specs=[pl.BlockSpec(shape, mine)] * 2 + untouched(deps),
            out_specs=[block, block],
        ),
        out_shape=[
            jax.ShapeDtypeStruct(shape, jnp.float32),
            jax.ShapeDtypeStruct(shape, jnp.bfloat16),
        ],
        compiler_params=params(),
        cost_estimate=cheap(),
        name="chip_state",
    )(info, exact, other, *deps)


def join_kernel(start, last, chip_ref, before_ref, arrived_ref, *rest):
    chip_out, before_out, sent_ref = rest[-3:]
    arrived = opened(arrived_ref[...])
    before = arrived if start else joined(arrived, before_ref[...])
    before_out[...] = before
    if last:
        sent_ref[...] = closed(before)
    else:
        chip = joined(arrived, chip_ref[...])
        chip_out[...] = chip
        sent_ref[...] = closed(chip)


def join(chip, before, arrived, start, last, deps):
    block = pl.BlockSpec(chip.shape, lambda b: (0, 0, 0))
    return pl.pallas_call(
        functools.partial(join_kernel, start, last),
        grid=(1,),
        in_specs=[block] * 3 + untouched(deps),
        out_specs=[block] * 3,
        out_shape=[
            jax.ShapeDtypeStruct(chip.shape, jnp.float32),
            jax.ShapeDtypeStruct(chip.shape, jnp.float32),
            jax.ShapeDtypeStruct(chip.shape, jnp.bfloat16),
        ],
        compiler_params=params(),
        cost_estimate=cheap(),
        name="join",
    )(chip, before, arrived, *deps)


def mix_local_kernel(query_ref, key_ref, value_ref, col_ref, row_ref, first_ref, *rest):
    out_ref = rest[-1]
    rows = query_ref.shape[0]
    key_at = lax.broadcasted_iota(jnp.int32, (SUB, SUB), 0)
    query_at = lax.broadcasted_iota(jnp.int32, (SUB, SUB), 1)
    causal = key_at <= query_at
    value_t, query_t = value_ref[...].T, query_ref[...].T
    for at in range(0, rows, SUB):
        here = slice(at, at + SUB)
        for head, (start, width, place) in enumerate(WINDOWS):
            lanes = slice(start, start + width)
            features = slice(head * DH, (head + 1) * DH)
            query = query_ref[here, lanes]
            query = jnp.where(head_lanes(query.shape, place), query, jnp.zeros_like(query))
            score = lax.dot_general(
                key_ref[here, lanes],
                query,
                (((1,), (1,)), ((), ())),
                preferred_element_type=jnp.float32,
            )
            along = row_ref[0, head : head + 1, here]
            gap = jnp.where(causal, along - col_ref[0, here, head : head + 1], -jnp.inf)
            mixing = (score * jnp.exp(gap)).astype(jnp.bfloat16)
            result = jnp.dot(value_t[features, here], mixing, preferred_element_type=jnp.float32)
            if at:
                since = along - row_ref[0, head : head + 1, at - 1 : at]
                scaled = query_t[features, here].astype(jnp.float32) * jnp.exp(since)
                result = result + jnp.dot(
                    first_ref[head][:, :DH].astype(jnp.bfloat16),
                    scaled.astype(jnp.bfloat16),
                    preferred_element_type=jnp.float32,
                )
            out_ref[features, here] = result


def mix_local(query, key, value, decay_cols, decay_rows, first, deps):
    rows, width = query.shape
    block = pl.BlockSpec((rows, WIDE), lambda b: (0, b))
    return pl.pallas_call(
        mix_local_kernel,
        grid=(width // WIDE,),
        in_specs=[
            block,
            block,
            block,
            pl.BlockSpec((1, rows, BUNDLE), lambda b: (b, 0, 0)),
            pl.BlockSpec((1, BUNDLE, rows), lambda b: (b, 0, 0)),
            pl.BlockSpec((BUNDLE, DH, LANES), lambda b: (b, 0, 0)),
        ]
        + untouched(deps),
        out_specs=pl.BlockSpec((WIDE, rows), lambda b: (b, 0)),
        out_shape=jax.ShapeDtypeStruct((width, rows), jnp.float32),
        compiler_params=params(),
        cost_estimate=cheap(),
        name="mix_local",
    )(query, key, value, decay_cols, decay_rows, first, *deps)


def mix_final_kernel(half, info, query_ref, local_ref, row_ref, own_ref, sent_ref, other_ref, *rest):
    out_ref = rest[-1]
    core = lax.rem(info[0], 2)
    mine = (pl.program_id(0) >= half).astype(jnp.int32) == core
    query_t = query_ref[...].T
    heads = []
    for head in range(BUNDLE):
        features = slice(head * DH, (head + 1) * DH)
        state = jnp.where(mine, own_ref[head], opened(sent_ref[head]))
        state = jnp.where(core == 0, state, joined(state, opened(other_ref[head])))
        scaled = query_t[features, :].astype(jnp.float32) * jnp.exp(row_ref[0, head : head + 1, :])
        result = local_ref[features, :] + jnp.dot(
            state[:, :DH].astype(jnp.bfloat16),
            scaled.astype(jnp.bfloat16),
            preferred_element_type=jnp.float32,
        )
        square = jnp.sum(result * result, axis=0, keepdims=True) * (1.0 / DH)
        heads.append(result * lax.rsqrt(square + EPS_NORM))
    out_ref[...] = jnp.concatenate(heads, axis=0).T.astype(out_ref.dtype)


def mix_final(info, query, local, decay_rows, own, sent, other, deps):
    rows, width = query.shape
    bundles = width // WIDE
    half = bundles // 2
    block = pl.BlockSpec((rows, WIDE), lambda b, _: (0, b))
    states = pl.BlockSpec((BUNDLE, DH, LANES), lambda b, _: (b, 0, 0))
    halves = pl.BlockSpec((BUNDLE, DH, LANES), lambda b, _: (lax.rem(b, half), 0, 0))
    return pl.pallas_call(
        functools.partial(mix_final_kernel, half),
        grid_spec=pltpu.PrefetchScalarGridSpec(
            num_scalar_prefetch=1,
            grid=(bundles,),
            in_specs=[
                block,
                pl.BlockSpec((WIDE, rows), lambda b, _: (b, 0)),
                pl.BlockSpec((1, BUNDLE, rows), lambda b, _: (b, 0, 0)),
                halves,
                halves,
                states,
            ]
            + untouched(deps),
            out_specs=block,
        ),
        out_shape=jax.ShapeDtypeStruct((rows, width), jnp.bfloat16),
        compiler_params=params(),
        cost_estimate=cheap(),
        name="mix_final",
    )(info, query, local, decay_rows, own, sent, other, *deps)


def group_sizes(bundles):
    if bundles == 8:
        return [2, 3, 2, 1]
    return [1] * bundles


def per_device(query1, key1, value1, log_decay, out_weight, query2, key2, value2):
    rows, width = query1.shape
    bundles = width // WIDE
    count = lax.axis_size("ctx")
    position = lax.axis_index("ctx")
    info = jnp.full((1,), position, jnp.int32)

    def moved(value, pairs):
        return lax.ppermute(value, "ctx", [(s, t) for s, t in pairs if 0 <= t < count])

    everyone = range(count)
    step_pairs = [(s, s + 3 if s % 2 else s + 1) for s in everyone]
    chip_pairs = [(s, s + 2) for s in everyone if s % 4 != 3]
    back_pairs = [(s, s - 1) for s in everyone if s % 4 == 2 and s > 2]
    swap_pairs = [(s, s ^ 1) for s in everyone]

    sizes = group_sizes(bundles)
    groups = len(sizes)
    bases = [sum(sizes[:g]) for g in range(groups)]
    near, chip, back, mid, swap = {}, {}, {}, {}, {}
    done = {"last": [], "attended": None}

    def do_pack(group):
        if group < groups:
            sent = pack(key2, value2, bases[group], sizes[group], done["last"])
            near[group] = moved(sent, step_pairs)
            chip[group] = moved(sent, chip_pairs)
            done["last"] = [sent]

    def do_back(group):
        if group < groups:
            near[group] = gate(near[group], done["last"])
            done["last"] = [near[group]]
            back[group] = moved(near[group], back_pairs)

    def do_pick(group):
        if group < groups:
            mid[group] = pick(info, chip[group], back[group], done["last"])
            swap[group] = moved(mid[group], swap_pairs)
            done["last"] = [mid[group]]

    def do_attend(group):
        if group < groups:
            done["attended"] = attend(
                info, query2, key2, value2, near[group], mid[group], swap[group],
                done["attended"], bases[group],
                [array for array in done["last"] if array is not done["attended"]],
            )
            done["last"] = [done["attended"]]

    light = {"distance": 1, "before": None}

    def do_state():
        running = jnp.cumsum(log_decay, axis=0)
        light["cols"] = running.reshape(rows, bundles, BUNDLE).transpose(1, 0, 2)
        light["rows"] = running.T.reshape(bundles, BUNDLE, rows)
        exact, first, sent = local_state(key1, value1, light["rows"], done["last"])
        light["first"] = first
        light["other"] = moved(sent, swap_pairs)
        light["exact"] = exact
        done["last"] = [sent]

    def do_chip():
        light["chip"], sent = chip_state(info, light["exact"], light["other"], done["last"])
        light["arrived"] = moved(sent, [(s, s + 2) for s in everyone])
        light["distance"] = 1
        done["last"] = [sent]

    def do_join():
        if light["distance"] < count // 2:
            start = light["distance"] == 1
            light["distance"] *= 2
            last = light["distance"] >= count // 2
            before = light["chip"] if start else light["before"]
            light["chip"], light["before"], sent = join(
                light["chip"], before, light["arrived"], start, last, done["last"]
            )
            pairs = swap_pairs if last else [(s, s + 2 * light["distance"]) for s in everyone]
            light["arrived"] = moved(sent, pairs)
            done["last"] = [sent]

    def do_mix_local():
        light["local"] = mix_local(
            query1, key1, value1, light["cols"], light["rows"], light["first"], done["last"]
        )
        done["last"] = [light["local"]]

    def do_mix_final():
        while light["distance"] < count // 2:
            do_join()
        light["normed"] = mix_final(
            info, query1, light["local"], light["rows"], light["before"], light["arrived"],
            light["other"], done["last"],
        )
        done["last"] = [light["normed"]]

    def do_project():
        product = jnp.dot(light["normed"], out_weight, preferred_element_type=jnp.float32)
        product = product.astype(jnp.bfloat16)
        done["linear"] = lax.psum_scatter(product, "head", scatter_dimension=0, tiled=True)
        done["last"] = [product]

    def wait_chip(group):
        if group < groups:
            done["last"] = done["last"] + [chip[group]]

    do_pack(0)
    do_pack(1)
    do_state()
    do_mix_local()
    do_back(0)
    wait_chip(0)
    do_chip()
    do_pick(0)
    do_join()
    do_back(1)
    do_attend(0)
    wait_chip(1)
    do_join()
    do_pack(2)
    do_pick(1)
    do_join()
    do_pack(3)
    wait_chip(2)
    do_mix_final()
    do_back(2)
    do_project()
    do_back(3)
    do_pick(2)
    do_attend(1)
    do_pick(3)
    do_attend(2)
    do_attend(3)
    return (done["linear"], done["attended"])


def solution(mesh):
    in_specs = (
        P("ctx", "head"),
        P("ctx", "head"),
        P("ctx", "head"),
        P("ctx", "head"),
        P("head", None),
        P("ctx", "head"),
        P("ctx", "head"),
        P("ctx", "head"),
    )
    out_specs = (P(("ctx", "head"), None), P("ctx", "head"))
    return jax.shard_map(
        per_device, mesh=mesh, in_specs=in_specs, out_specs=out_specs, check_vma=False
    )
```
